256 devices in a mesh: blk: 32 (over z, y_lo, core), rep: 8 (over x, y_hi).
Axes of the slice: x: 4, y: 4 (y_hi: 2, y_lo: 2; y = y_hi * 2 + y_lo), z: 8, core: 2. Of those that a mesh axis runs over, the one named last changes fastest.
Arguments:
- features: bfloat16 [32768, 128], P('blk'), may hold values from -6 to 6
- degrees: int32 [32768], P('blk'), may hold values from 4 to 32
- slot_column_tiles: int32 [256, 32, 6], P('blk', 'rep'), may hold values from 0 to 7
- tile_counts: int32 [256, 32], P('blk', 'rep'), may hold values from 0 to 6, as said below
- slot_edge_weights: bfloat16 [256, 32, 6, 128, 128], P('blk', 'rep'), may hold values from 0 to 0.15234375
- weight: bfloat16 [128, 256], replicated, may hold values from -0.5 to 0.5
- bias: float32 [256], replicated, may hold values from -3 to 3
- cotangent: bfloat16 [32768, 256], P(('blk', 'rep')), may hold values from -1.1953125 to 1.1953125
Outputs:
- activation: bfloat16 [32768, 256], P(('blk', 'rep'))
- grad_weight: float32 [128, 256], replicated
- grad_bias: float32 [256], replicated
- grad_features: float32 [32768, 128], P(('blk', 'rep'))
The draws below stay inside these ranges and needn't reach their ends.
Inputs may be any that keep to these rules, and one draw needn't show every extreme that they name: slot_column_tiles[i, g, c] names a tile of node block (i // 8 - g) mod 32. Slots c >= tile_counts[i, g] of row tile i at offset g are not part of A; 6 is reached in every draw.
All inputs are finite; a program needn't handle non-finite values.
Results may differ from the reference program's by a relative error of at most 0.025.
Values may be sent and summed in bfloat16 or wider, within the bound.
No kernel may reach another device: no remote copies, remote signals or barrier semaphores. Data moves between devices by JAX's collectives and lax.ppermute only.
A program may use at most 64 MiB of HBM per device.

```python
import jax
import jax.numpy as jnp
from jax import lax

FIN = 128
FOUT = 256
TILE_NODES = 128
BLOCK_ROW_TILES = 8
SLOTS_PER_OFFSET = 6
TOTAL_TILES = 256
NODES = 32768
N_BLK = 32


def draw_tile_counts(key, part):
    key = jax.random.fold_in(key, 7)
    subkeys = jax.random.split(key, 5)
    tile_load_level = jax.random.randint(subkeys[0], (N_BLK,), 0, 3)
    busiest = jax.random.randint(subkeys[1], (), 0, N_BLK)
    tile_load_level = jnp.where(jnp.arange(N_BLK) == busiest, 0, tile_load_level)
    slot_capacity = jnp.maximum(SLOTS_PER_OFFSET // jnp.left_shift(1, tile_load_level), 1)
    cap_rows = jnp.repeat(slot_capacity, BLOCK_ROW_TILES)
    raw_draw = jax.random.randint(subkeys[2], (TOTAL_TILES, N_BLK), 0, 1 << 20)
    counts = raw_draw % (cap_rows[:, None] + 1)
    pick_row = jax.random.randint(subkeys[3], (N_BLK,), 0, BLOCK_ROW_TILES)
    pick_off = jax.random.randint(subkeys[4], (N_BLK,), 0, N_BLK)
    row_ids = jnp.arange(TOTAL_TILES)
    owner = row_ids // BLOCK_ROW_TILES
    row_forced = row_ids % BLOCK_ROW_TILES == pick_row[owner]
    off_forced = jnp.arange(N_BLK)[None, :] == pick_off[owner][:, None]
    is_forced = row_forced[:, None] & off_forced
    counts = jnp.where(is_forced, cap_rows[:, None], counts)
    return counts.astype(jnp.int32)


def set_ends(values, own_key, smallest, top_value):
    spot = [jax.random.randint(jax.random.fold_in(own_key, axis), (), 0, length) for axis, length in enumerate(values.shape)]
    longest = values.shape.index(max(values.shape))
    neighbour = spot[:longest] + [(spot[longest] + 1) % values.shape[longest]] + spot[longest + 1:]
    return values.at[tuple(spot)].set(smallest).at[tuple(neighbour)].set(top_value)


def block_scale(rng, dims, pieces, smallest, top_value):
    gain = 1.0
    for axis_at, shards_of in pieces:
        heights = jax.random.uniform(jax.random.fold_in(jax.random.fold_in(rng, 6), axis_at), (shards_of,), jnp.float32, smallest / len(pieces), top_value / len(pieces))
        gain = gain * jnp.repeat(jnp.exp(heights), dims[axis_at] // shards_of).reshape((-1,) + (1,) * (len(dims) - 1 - axis_at))
    return gain


def gaussian(own_key, shape, deviation, most, pieces=(), kind=jnp.bfloat16):
    loudness = block_scale(own_key, shape, pieces, -0.22, 0.18) if pieces else 1.0
    drawn = jax.random.normal(own_key, shape, jnp.float32) * deviation * loudness
    return jnp.minimum(jnp.maximum(drawn, -most), most).astype(kind)


def setup_inputs(seed: int = 0) -> dict:
    key_list = jax.random.split(jax.random.key(seed), 9)
    return {
        "features": gaussian(key_list[0], (NODES, FIN), 1.0, 6.0, ((0, 32),)),
        "degrees": set_ends(jax.random.randint(key_list[1], (NODES,), 4, 33), jax.random.fold_in(key_list[1], 1), 4, 32).astype(jnp.int32),
        "slot_column_tiles": set_ends(jax.random.randint(key_list[2], (TOTAL_TILES, N_BLK, SLOTS_PER_OFFSET), 0, BLOCK_ROW_TILES), jax.random.fold_in(key_list[2], 1), 0, BLOCK_ROW_TILES - 1).astype(jnp.int32),
        "tile_counts": draw_tile_counts(jax.random.fold_in(key_list[8], 71), 0),
        "slot_edge_weights": jnp.clip(0.15234375 * jax.random.uniform(key_list[4], (TOTAL_TILES, N_BLK, SLOTS_PER_OFFSET, TILE_NODES, TILE_NODES), jnp.float32) ** block_scale(key_list[4], (TOTAL_TILES, N_BLK, SLOTS_PER_OFFSET, TILE_NODES, TILE_NODES), ((0, 32), (1, 8)), -0.2, 0.2), 0.0, 0.15234375).astype(jnp.bfloat16),
        "weight": gaussian(key_list[5], (FIN, FOUT), FIN ** -0.5, 0.5),
        "bias": gaussian(key_list[6], (FOUT,), 0.5, 3.0, (), jnp.float32),
        "cotangent": gaussian(key_list[7], (NODES, FOUT), 0.2, 1.1953125, ((0, 256),)),
    }


def reference(features, degrees, slot_column_tiles, tile_counts, slot_edge_weights, weight, bias, cotangent):
    inv_root = lax.rsqrt(degrees.astype(jnp.float32))
    scaled = (features * inv_root[:, None]).astype(jnp.bfloat16)
    feat_tiles = scaled.reshape(N_BLK * BLOCK_ROW_TILES, TILE_NODES, FIN)
    offsets = jnp.arange(N_BLK, dtype=jnp.int32)
    slot_numbers = jnp.arange(SLOTS_PER_OFFSET, dtype=jnp.int32)
    block_ids = jnp.arange(N_BLK, dtype=jnp.int32)
    column_block_list = slot_column_tiles.reshape(N_BLK, BLOCK_ROW_TILES, N_BLK, SLOTS_PER_OFFSET)
    count_blocks = tile_counts.reshape(N_BLK, BLOCK_ROW_TILES, N_BLK)
    edge_weight_blocks = slot_edge_weights.reshape(N_BLK, BLOCK_ROW_TILES, N_BLK, SLOTS_PER_OFFSET, TILE_NODES, TILE_NODES)

    def column_tiles(block_idx, col_ids):
        position = (block_idx - offsets) % N_BLK
        return (position[None, :, None] * BLOCK_ROW_TILES + col_ids).astype(jnp.int32)

    def forward_block(packed):
        block_idx, col_ids, counts, edge_vals = packed
        live_mask = slot_numbers[None, None, :] < counts[:, :, None]
        picked = feat_tiles[column_tiles(block_idx, col_ids)].astype(jnp.float32)
        picked = jnp.where(live_mask[:, :, :, None, None], picked, jnp.zeros_like(picked))
        return jnp.einsum('igsab,igsbf->iaf', edge_vals.astype(jnp.float32), picked)
    sums = lax.map(forward_block, (block_ids, column_block_list, count_blocks, edge_weight_blocks))
    aggregate = (inv_root[:, None] * sums.reshape(N_BLK * BLOCK_ROW_TILES * TILE_NODES, FIN)).astype(jnp.bfloat16)
    pre_act = jnp.dot(aggregate, weight, preferred_element_type=jnp.float32) + bias
    activation = jax.nn.silu(pre_act).astype(jnp.bfloat16)
    sigma = jax.nn.sigmoid(pre_act)
    grad_pre = cotangent.astype(jnp.float32) * sigma * (1.0 + pre_act * (1.0 - sigma))
    grad_half = grad_pre.astype(jnp.bfloat16)
    grad_weight = lax.dot_general(aggregate, grad_half, (((0,), (0,)), ((), ())), preferred_element_type=jnp.float32)
    grad_bias = lax.optimization_barrier(jnp.sum(grad_pre, axis=0))
    back_full = lax.dot_general(grad_half, weight, (((1,), (1,)), ((), ())), preferred_element_type=jnp.float32)
    back = (inv_root[:, None] * back_full).astype(jnp.bfloat16)
    back_blocks = back.reshape(N_BLK, BLOCK_ROW_TILES, TILE_NODES, FIN)

    def backward_block(running, packed):
        block_idx, col_ids, counts, edge_vals, back_rows = packed
        live_mask = slot_numbers[None, None, :] < counts[:, :, None]
        terms = jnp.einsum('igsab,iaf->igsbf', edge_vals.astype(jnp.float32), back_rows.astype(jnp.float32))
        terms = jnp.where(live_mask[:, :, :, None, None], terms, jnp.zeros_like(terms))
        targets = column_tiles(block_idx, col_ids).reshape(-1)
        running = running.at[targets].add(terms.reshape(-1, TILE_NODES, FIN))
        return (running, None)
    initial = jnp.zeros((N_BLK * BLOCK_ROW_TILES, TILE_NODES, FIN), jnp.float32)
    column_sums, _ = lax.scan(backward_block, initial, (block_ids, column_block_list, count_blocks, edge_weight_blocks, back_blocks))
    grad_features = inv_root[:, None] * column_sums.reshape(N_BLK * BLOCK_ROW_TILES * TILE_NODES, FIN)
    return (activation, grad_weight, grad_bias, grad_features)
```

```python
import jax
import jax.numpy as jnp
from jax import lax
from jax.experimental import pallas as pl
from jax.experimental.pallas import tpu as pltpu
from jax.sharding import Mesh
from jax.sharding import PartitionSpec as P

Z, YL, CORE, X, YH = 8, 2, 2, 4, 2
BLK = ("z", "yl", "core")
REP = ("x", "yh")
T = 128
ROWS = 8
STEPS = 4
SLOTS = 6
GRAD = 48
F32 = jnp.float32
BF16 = jnp.bfloat16

VMEM = pl.BlockSpec(memory_space=pltpu.VMEM)
SMEM = pl.BlockSpec(memory_space=pltpu.SMEM)
PARAMS = pltpu.CompilerParams(vmem_limit_bytes=32 * 1024 * 1024)


def bias_rows(total):
    high = total.astype(BF16)
    low = (total - high.astype(F32)).astype(BF16)
    return jnp.concatenate([high, low, jnp.zeros((12, T), BF16)], axis=0)


def bias_of(rows):
    rows = rows.astype(F32)
    return rows[0:2] + rows[2:4]


def forward_kernel(cols, counts, odd, edges, own, far, near0, near1, out):
    i = pl.program_id(0)
    is_odd = odd[0] == 1
    total = jnp.zeros((T, T), F32)
    for s in range(STEPS):
        picked = []
        for c in range(SLOTS):
            col = cols[i, s, c]
            if s == 0:
                tile = own[col, 0]
            elif s == 2:
                tile = far[col]
            elif s == 1:
                tile = jnp.where(is_odd, near0[col], near1[col])
            else:
                tile = jnp.where(is_odd, near1[col], near0[col])
            picked.append(jnp.where(c < counts[i, s], tile, jnp.zeros_like(tile)))
        left = jnp.concatenate([edges[0, s, c] for c in range(SLOTS)], axis=1)
        total += jnp.dot(left, jnp.concatenate(picked, axis=0), preferred_element_type=F32)
    out[0] = total.astype(BF16)


def dense_kernel(parts, scale, weight, bias, cot, act, send):
    total = parts[0].astype(F32)
    for j in range(1, ROWS):
        total += parts[j].astype(F32)
    agg = (scale[...] * total).astype(BF16)
    pre = jnp.dot(agg, weight[...], preferred_element_type=F32) + bias[...]
    sigma = jax.nn.sigmoid(pre)
    act[...] = (pre * sigma).astype(BF16)
    grad_pre = cot[...].astype(F32) * sigma * (1.0 + pre * (1.0 - sigma))
    half = grad_pre.astype(BF16)
    grad_w = lax.dot_general(agg, half, (((0,), (0,)), ((), ())), preferred_element_type=F32)
    grad_b = jnp.sum(grad_pre, axis=0, keepdims=True)
    grad_b = jnp.concatenate([grad_b[:, :T], grad_b[:, T:]], axis=0)
    back = lax.dot_general(
        half, weight[...], (((1,), (1,)), ((), ())), preferred_element_type=F32
    )
    back = (scale[...] * back).astype(BF16)
    rows_b = bias_rows(grad_b)
    grad_w = grad_w.astype(BF16)
    for j in range(ROWS):
        send[j, 0:T] = back
        send[j, T : T + 16] = grad_w[16 * j : 16 * j + 16, :T]
        send[j, T + 16 : T + 32] = grad_w[16 * j : 16 * j + 16, T:]
        send[j, T + 32 : T + 48] = rows_b


def backward_kernel(cols, counts, odd, edges, got, near, keep, far, grads, sums):
    i = pl.program_id(0)

    @pl.when(i == 0)
    def _():
        sums[...] = jnp.zeros_like(sums)
        total = got[0, T:].astype(F32)
        for j in range(1, ROWS):
            total += got[j, T:].astype(F32)
        grads[0:32] = total[0:32].astype(BF16)
        grads[32:48] = bias_rows(total[32:34] + total[34:36])

    back = got[i, 0:T].T
    for s in range(STEPS):
        right = jnp.concatenate([edges[0, s, c] for c in range(SLOTS)], axis=1)
        prod = jnp.dot(back, right, preferred_element_type=F32)
        for c in range(SLOTS):
            part = prod[:, c * T : (c + 1) * T]
            at = s * ROWS + cols[i, s, c]
            sums[at] += jnp.where(c < counts[i, s], part, jnp.zeros_like(part))

    @pl.when(i == ROWS - 1)
    def _():
        is_odd = odd[0] == 1
        one = sums[ROWS : 2 * ROWS].astype(BF16)
        three = sums[3 * ROWS :].astype(BF16)
        keep[...] = sums[0:ROWS].astype(BF16)
        far[...] = sums[2 * ROWS : 3 * ROWS].astype(BF16)
        near[0:ROWS] = jnp.where(is_odd, one, three)
        near[ROWS:] = jnp.where(is_odd, three, one)


def add_grads(a, b):
    total = a[0:32].astype(F32) + b[0:32].astype(F32)
    return jnp.concatenate([total.astype(BF16), bias_rows(bias_of(a[32:]) + bias_of(b[32:]))], 0)


def near_kernel(far, near_far, grads, near_grads, out, out_grads):
    out[...] = (far[...].astype(F32) + near_far[...].astype(F32)).astype(BF16)
    out_grads[...] = add_grads(grads[...], near_grads[...])


def far_kernel(where_at, keep, near, far, grads, far_grads, out, out_grads):
    even, low = where_at[0] == 0, where_at[1] == 0
    near_f, far_f = near[...].astype(F32), far[...].astype(F32)
    zero = jnp.zeros_like(near_f)
    first = keep[...].astype(F32) + jnp.where(even, near_f, zero) + jnp.where(low, far_f, zero)
    second = jnp.where(even, zero, near_f) + jnp.where(low, zero, far_f)
    total = add_grads(grads[...], far_grads[...])
    out_grads[...] = total
    for j in range(ROWS):
        out[j, 0:T] = first[j].astype(BF16)
        out[j, T : 2 * T] = second[j].astype(BF16)
        out[j, 2 * T :] = total[0:32]


def turn_kernel(where_at, got, grads, out):
    even, z = where_at[0] == 0, where_at[2]
    half = []
    for j in range(ROWS):
        half.append(jnp.where(even, got[j, 2 * T : 2 * T + 16], got[j, 2 * T + 16 :]))
    half = jnp.concatenate(half, axis=0)
    for p in range(Z):
        d = lax.rem(z - p + Z, Z)
        before = lax.rem(d + Z - 1, Z)
        out[p, 0:T] = (got[d, 0:T].astype(F32) + got[before, T : 2 * T].astype(F32)).astype(BF16)
        out[p, T : 2 * T] = half
        out[p, 2 * T :] = grads[32:48]


def last_kernel(got, scale, grad_features, grad_half, grad_bias):
    total = got[0].astype(F32)
    for p in range(1, Z):
        total += got[p].astype(F32)
    grad_features[...] = scale[...] * total[0:T].T
    grad_half[...] = total[T : 2 * T]
    bias = total[2 * T : 2 * T + 2] + total[2 * T + 2 : 2 * T + 4]
    grad_bias[...] = jnp.concatenate([bias[0:1], bias[1:2]], axis=1)


def call(kernel, out, in_specs):
    return pl.pallas_call(
        kernel,
        out_shape=[jax.ShapeDtypeStruct(*o) for o in out],
        in_specs=in_specs,
        out_specs=[VMEM] * len(out),
        compiler_params=PARAMS,
    )


def whole(shape):
    return pl.BlockSpec(shape, lambda i: (0,) * len(shape))


EDGES = pl.BlockSpec((1, STEPS, SLOTS, T, T), lambda i: (i, 0, 0, 0, 0))


def exchange(value, axes):
    return lax.all_to_all(value, axes, 0, 0, tiled=True)


def swap(value, axis):
    return lax.ppermute(value, axis, [(0, 1), (1, 0)])


def on_device(features, degrees, cols, counts, edges, weight, bias, cot):
    z, yl, core = (lax.axis_index(a) for a in BLK)
    rep = lax.axis_index(REP)
    even, low = core == 0, yl == 0
    own_degrees = lax.dynamic_slice_in_dim(degrees, rep * T, T, 0)
    scale = jnp.broadcast_to(lax.rsqrt(own_degrees.astype(F32))[:, None], (T, T))
    own = lax.dynamic_slice_in_dim(features, rep * T, T, 0)
    own = (own * scale).astype(BF16)
    odd = core.astype(jnp.int32)[None]
    where_at = jnp.stack([core, yl, z]).astype(jnp.int32)

    planes = exchange(jnp.broadcast_to(own[None], (Z, T, T)), "z")
    wanted = (z - jnp.arange(ROWS)[:, None] - jnp.arange(2)[None, :]) % Z
    own = exchange(planes[wanted], REP)
    far = swap(jnp.where(low, own[:, 0], own[:, 1]), "yl")
    near0 = swap(jnp.where(even, own[:, 0], own[:, 1]), "core")
    near1 = swap(far, "core")

    tiles = (ROWS, T, T)
    (parts,) = pl.pallas_call(
        forward_kernel,
        grid=(ROWS,),
        out_shape=[jax.ShapeDtypeStruct(tiles, BF16)],
        in_specs=[SMEM, SMEM, SMEM, EDGES, whole((ROWS, 2, T, T))] + [whole(tiles)] * 3,
        out_specs=[pl.BlockSpec((1, T, T), lambda i: (i, 0, 0))],
        compiler_params=PARAMS,
    )(cols, counts, odd, edges, own, far, near0, near1)
    parts = exchange(parts, REP)

    act, send = call(
        dense_kernel,
        [(cot.shape, BF16), ((ROWS, T + GRAD, T), BF16)],
        [VMEM] * 5,
    )(parts, scale, weight, bias[None], cot)
    got = exchange(send, REP)

    near, keep, far, grads = pl.pallas_call(
        backward_kernel,
        grid=(ROWS,),
        out_shape=[
            jax.ShapeDtypeStruct((2 * ROWS, T, T), BF16),
            jax.ShapeDtypeStruct(tiles, BF16),
            jax.ShapeDtypeStruct(tiles, BF16),
            jax.ShapeDtypeStruct((GRAD, T), BF16),
        ],
        in_specs=[SMEM, SMEM, SMEM, EDGES, whole((ROWS, T + GRAD, T))],
        out_specs=[whole((2 * ROWS, T, T)), whole(tiles), whole(tiles), whole((GRAD, T))],
        scratch_shapes=[pltpu.VMEM((STEPS * ROWS, T, T), F32)],
        compiler_params=PARAMS,
    )(cols, counts, odd, edges, got)

    near = swap(near, "core")
    near_grads = swap(grads, "core")
    far, grads = call(near_kernel, [(tiles, BF16), ((GRAD, T), BF16)], [VMEM] * 4)(
        far, near[ROWS:], grads, near_grads
    )
    far_got, far_grads = swap(far, "yl"), swap(grads, "yl")
    send, grads = call(
        far_kernel,
        [((ROWS, 2 * T + 32, T), BF16), ((GRAD, T), BF16)],
        [SMEM] + [VMEM] * 5,
    )(where_at, keep, near[:ROWS], far_got, grads, far_grads)
    got = exchange(send, REP)
    (send,) = call(turn_kernel, [((Z, 2 * T + 16, T), BF16)], [SMEM, VMEM, VMEM])(
        where_at, got, grads
    )
    got = exchange(send, "z")
    grad_features, half, grad_bias = call(
        last_kernel,
        [((T, T), F32), ((T, T), F32), ((1, 2 * T), F32)],
        [VMEM, VMEM],
    )(got, scale)
    other = swap(half, "core")
    grad_weight = jnp.concatenate(
        [jnp.where(even, half, other), jnp.where(even, other, half)], axis=1
    )
    return act, grad_weight, grad_bias[0], grad_features


def solution(mesh):
    fine = Mesh(mesh.devices.reshape(Z, YL, CORE, X, YH), BLK + REP)
    return jax.shard_map(
        on_device,
        mesh=fine,
        in_specs=(
            P(BLK, None),
            P(BLK),
            P(BLK, REP, None),
            P(BLK, REP),
            P(BLK, REP, None, None, None),
            P(),
            P(),
            P(BLK + REP, None),
        ),
        out_specs=(P(BLK + REP, None), P(), P(), P(BLK + REP, None)),
        check_vma=False,
    )
```

```python
import functools

import jax
import jax.numpy as jnp
from jax import lax
from jax.experimental import pallas as pl
from jax.experimental.pallas import tpu as pltpu
from jax.sharding import Mesh
from jax.sharding import PartitionSpec as P

Z, YL, CORE, X, YH = 8, 2, 2, 4, 2
BLK = ("z", "yl", "core")
REP = ("x", "yh")
T = 128
ROWS = 8
STEPS = 4
SLOTS = 6
GRAD = 48
F32 = jnp.float32
BF16 = jnp.bfloat16

VMEM = pl.BlockSpec(memory_space=pltpu.VMEM)
SMEM = pl.BlockSpec(memory_space=pltpu.SMEM)
HBM = pl.BlockSpec(memory_space=pltpu.HBM)
PARAMS = pltpu.CompilerParams(vmem_limit_bytes=32 * 1024 * 1024)


def bias_rows(total):
    high = total.astype(BF16)
    low = (total - high.astype(F32)).astype(BF16)
    return jnp.concatenate([high, low, jnp.zeros((12, T), BF16)], axis=0)


def bias_of(rows):
    rows = rows.astype(F32)
    return rows[0:2] + rows[2:4]


def prologue_kernel(rep, features, degrees, planes, scale):
    row = degrees[pl.ds(rep[0], 1), :].astype(F32)
    diagonal = lax.broadcasted_iota(jnp.int32, (T, T), 0) == lax.broadcasted_iota(
        jnp.int32, (T, T), 1
    )
    column = jnp.sum(jnp.where(diagonal, row, jnp.zeros((T, T), F32)), axis=1, keepdims=True)
    inv_root = jnp.broadcast_to(lax.rsqrt(column), (T, T))
    scale[...] = inv_root
    own = (features[...].astype(F32) * inv_root).astype(BF16)
    for p in range(Z):
        planes[p] = own


def planes_kernel(meta, planes, out):
    z = meta[7, 0, 2]
    for j in range(ROWS):
        out[j, 0] = planes[lax.rem(z - j + Z, Z)]
        out[j, 1] = planes[lax.rem(z - j - 1 + Z, Z)]


def pick_kernel(which, meta, own, out):
    at = meta[7, 0, which]
    for j in range(ROWS):
        out[j] = own[j, at]


def product(meta, edges, i, s, tile_at):
    picked = []
    for c in range(SLOTS):
        tile = tile_at(meta[c, s, i])
        picked.append(jnp.where(c < meta[6, s, i], tile, jnp.zeros_like(tile)))
    left = jnp.concatenate([edges[i, s, c] for c in range(SLOTS)], axis=1)
    return jnp.dot(left, jnp.concatenate(picked, axis=0), preferred_element_type=F32)


def first_kernel(meta, edges, own, near, held, out, sems):
    copies = [pltpu.make_async_copy(edges.at[i], held.at[i], sems.at[i]) for i in range(ROWS)]
    for copy in copies:
        copy.start()
    step = 3 - 2 * meta[7, 0, 0]
    for i in range(ROWS):
        copies[i].wait()
        out[i] = product(meta, held, i, 0, lambda col: own[col, 0]) + product(
            meta, held, i, step, lambda col: near[col]
        )


def second_kernel(meta, held, far, total, out):
    for i in range(ROWS):
        out[i] = total[i] + product(meta, held, i, 2, lambda col: far[col])


def third_kernel(meta, held, near, total, out):
    step = 1 + 2 * meta[7, 0, 0]
    for i in range(ROWS):
        out[i] = (total[i] + product(meta, held, i, step, lambda col: near[col])).astype(BF16)


def dense_kernel(parts, scale, weight, bias, cot, act, send):
    total = parts[0].astype(F32)
    for j in range(1, ROWS):
        total += parts[j].astype(F32)
    agg = (scale[...] * total).astype(BF16)
    pre = jnp.dot(agg, weight[...], preferred_element_type=F32) + bias[...]
    sigma = jax.nn.sigmoid(pre)
    act[...] = (pre * sigma).astype(BF16)
    grad_pre = cot[...].astype(F32) * sigma * (1.0 + pre * (1.0 - sigma))
    half = grad_pre.astype(BF16)
    grad_w = lax.dot_general(agg, half, (((0,), (0,)), ((), ())), preferred_element_type=F32)
    grad_b = jnp.sum(grad_pre, axis=0, keepdims=True)
    grad_b = jnp.concatenate([grad_b[:, :T], grad_b[:, T:]], axis=0)
    back = lax.dot_general(
        half, weight[...], (((1,), (1,)), ((), ())), preferred_element_type=F32
    )
    back = (scale[...] * back).astype(BF16)
    rows_b = bias_rows(grad_b)
    grad_w = grad_w.astype(BF16)
    for j in range(ROWS):
        send[j, 0:T] = back
        send[j, T : T + 16] = grad_w[16 * j : 16 * j + 16, :T]
        send[j, T + 16 : T + 32] = grad_w[16 * j : 16 * j + 16, T:]
        send[j, T + 32 : T + 48] = rows_b


def column_sums(meta, held, got, s, sums):
    sums[...] = jnp.zeros_like(sums)
    for i in range(ROWS):
        back = got[i, 0:T].T
        right = jnp.concatenate([held[i, s, c] for c in range(SLOTS)], axis=1)
        prod = jnp.dot(back, right, preferred_element_type=F32)
        for c in range(SLOTS):
            part = prod[:, c * T : (c + 1) * T]
            at = meta[c, s, i]
            sums[at] += jnp.where(c < meta[6, s, i], part, jnp.zeros_like(part))


def near_sums_kernel(meta, held, got, near0, near1, grads, sums):
    total = got[0, T:].astype(F32)
    for j in range(1, ROWS):
        total += got[j, T:].astype(F32)
    grads[0:32] = total[0:32].astype(BF16)
    grads[32:48] = bias_rows(total[32:34] + total[34:36])
    column_sums(meta, held, got, 1 + 2 * meta[7, 0, 0], sums)
    near1[...] = sums[...].astype(BF16)
    column_sums(meta, held, got, 3 - 2 * meta[7, 0, 0], sums)
    near0[...] = sums[...].astype(BF16)


def far_sums_kernel(meta, held, got, far, sums):
    column_sums(meta, held, got, 2, sums)
    far[...] = sums[...].astype(BF16)


def own_sums_kernel(meta, held, got, near, out, sums):
    column_sums(meta, held, got, 0, sums)
    even = meta[7, 0, 0] == 0
    near_f = near[...].astype(F32)
    zero = jnp.zeros_like(near_f)
    out[0] = sums[...] + jnp.where(even, near_f, zero)
    out[1] = jnp.where(even, zero, near_f)


def add_grads(a, b):
    total = a[0:32].astype(F32) + b[0:32].astype(F32)
    return jnp.concatenate([total.astype(BF16), bias_rows(bias_of(a[32:]) + bias_of(b[32:]))], 0)


def near_kernel(far, near_far, grads, near_grads, out, out_grads):
    out[...] = (far[...].astype(F32) + near_far[...].astype(F32)).astype(BF16)
    out_grads[...] = add_grads(grads[...], near_grads[...])


def far_kernel(meta, own, far, grads, far_grads, out, out_grads):
    low = meta[7, 0, 1] == 0
    total = add_grads(grads[...], far_grads[...])
    out_grads[...] = total
    zero = jnp.zeros((T, T), F32)
    for j in range(ROWS):
        far_f = far[j].astype(F32)
        out[j, 0:T] = (own[0, j] + jnp.where(low, far_f, zero)).astype(BF16)
        out[j, T : 2 * T] = (own[1, j] + jnp.where(low, zero, far_f)).astype(BF16)
        out[j, 2 * T :] = total[0:32]


def turn_kernel(meta, got, grads, out):
    even, z = meta[7, 0, 0] == 0, meta[7, 0, 2]
    half = []
    for j in range(ROWS):
        half.append(jnp.where(even, got[j, 2 * T : 2 * T + 16], got[j, 2 * T + 16 :]))
    half = jnp.concatenate(half, axis=0)
    for p in range(Z):
        d = lax.rem(z - p + Z, Z)
        before = lax.rem(d + Z - 1, Z)
        out[p, 0:T] = (got[d, 0:T].astype(F32) + got[before, T : 2 * T].astype(F32)).astype(BF16)
        out[p, T : 2 * T] = half
        out[p, 2 * T :] = grads[32:48]


def last_kernel(got, scale, grad_features, grad_half, grad_bias):
    total = got[0].astype(F32)
    for p in range(1, Z):
        total += got[p].astype(F32)
    grad_features[...] = scale[...] * total[0:T].T
    grad_half[...] = total[T : 2 * T]
    bias = total[2 * T : 2 * T + 2] + total[2 * T + 2 : 2 * T + 4]
    grad_bias[...] = jnp.concatenate([bias[0:1], bias[1:2]], axis=1)


def call(kernel, out, in_specs, scratch=(), flops=0, moved=1 << 20):
    return pl.pallas_call(
        kernel,
        out_shape=[jax.ShapeDtypeStruct(*o) for o in out],
        in_specs=in_specs,
        out_specs=[VMEM] * len(out),
        scratch_shapes=list(scratch),
        cost_estimate=pl.CostEstimate(flops=flops, bytes_accessed=moved, transcendentals=0),
        compiler_params=PARAMS,
    )


def pinned(value):
    return pltpu.with_memory_space_constraint(value, pltpu.HBM)


def exchange(value, axes):
    return lax.all_to_all(value, axes, 0, 0, tiled=True)


def swap(value, axis):
    return lax.ppermute(value, axis, [(0, 1), (1, 0)])


def on_device(features, degrees, cols, counts, edges, weight, bias, cot):
    z, yl, core = (lax.axis_index(a) for a in BLK)
    rep = lax.axis_index(REP)
    even = core == 0
    place = lax.broadcasted_iota(jnp.int32, (1, STEPS, ROWS), 2)
    place = jnp.where(place == 0, core, jnp.where(place == 1, yl, z))
    meta = jnp.concatenate([cols.transpose(2, 1, 0), counts.T[None], place], axis=0)

    tiles = (ROWS, T, T)
    planes, scale = pl.pallas_call(
        prologue_kernel,
        grid_spec=pltpu.PrefetchScalarGridSpec(
            num_scalar_prefetch=1,
            grid=(1,),
            in_specs=[
                pl.BlockSpec((T, T), lambda i, rep: (rep[0], 0)),
                pl.BlockSpec((ROWS, T), lambda i, rep: (0, 0)),
            ],
            out_specs=[
                pl.BlockSpec((Z, T, T), lambda i, rep: (0, 0, 0)),
                pl.BlockSpec((T, T), lambda i, rep: (0, 0)),
            ],
        ),
        out_shape=[jax.ShapeDtypeStruct((Z, T, T), BF16), jax.ShapeDtypeStruct((T, T), F32)],
        compiler_params=PARAMS,
    )(rep.astype(jnp.int32)[None], pinned(features), pinned(degrees.reshape(ROWS, T)))
    planes = exchange(planes, "z")
    (own,) = call(planes_kernel, [((ROWS, 2, T, T), BF16)], [SMEM, VMEM])(meta, planes)
    own = exchange(own, REP)
    pick = [
        call(functools.partial(pick_kernel, which), [(tiles, BF16)], [SMEM, VMEM])
        for which in (0, 1)
    ]
    (far,) = pick[1](meta, own)
    far, own = lax.optimization_barrier((far, own))
    far = swap(far, "yl")
    near0 = swap(pick[0](meta, own)[0], "core")

    work = 2 * ROWS * SLOTS * T * T * T
    held, total = call(
        first_kernel,
        [(edges.shape, BF16), (tiles, F32)],
        [SMEM, HBM, VMEM, VMEM],
        [pltpu.SemaphoreType.DMA((ROWS,))],
        2 * work,
        8 << 20,
    )(meta, pinned(edges), own, near0)
    far, total = lax.optimization_barrier((far, total))
    near1 = swap(far, "core")
    (total,) = call(second_kernel, [(tiles, F32)], [SMEM] + [VMEM] * 3, (), work, 3 << 20)(
        meta, held, far, total
    )
    (parts,) = call(third_kernel, [(tiles, BF16)], [SMEM] + [VMEM] * 3, (), work, 3 << 20)(
        meta, held, near1, total
    )
    parts = exchange(parts, REP)

    act, send = call(
        dense_kernel,
        [(cot.shape, BF16), ((ROWS, T + GRAD, T), BF16)],
        [VMEM] * 5,
    )(parts, scale, weight, bias[None], cot)
    got = exchange(send, REP)

    sums = [pltpu.VMEM(tiles, F32)]
    near0, near1, grads = call(
        near_sums_kernel,
        [(tiles, BF16), (tiles, BF16), ((GRAD, T), BF16)],
        [SMEM, VMEM, VMEM],
        sums,
        2 * work,
        6 << 20,
    )(meta, held, got)
    near0, near1, near_grads = (swap(a, "core") for a in (near0, near1, grads))
    (far,) = call(far_sums_kernel, [(tiles, BF16)], [SMEM, VMEM, VMEM], sums, work, 3 << 20)(
        meta, held, got
    )
    far, grads = call(near_kernel, [(tiles, BF16), ((GRAD, T), BF16)], [VMEM] * 4)(
        far, near1, grads, near_grads
    )
    far, got = lax.optimization_barrier((far, got))
    far_got, far_grads = swap(far, "yl"), swap(grads, "yl")
    (own,) = call(
        own_sums_kernel, [((2, *tiles), F32)], [SMEM] + [VMEM] * 3, sums, work, 3 << 20
    )(meta, held, got, near0)
    send, grads = call(
        far_kernel,
        [((ROWS, 2 * T + 32, T), BF16), ((GRAD, T), BF16)],
        [SMEM] + [VMEM] * 4,
    )(meta, own, far_got, grads, far_grads)
    got = exchange(send, REP)
    (send,) = call(turn_kernel, [((Z, 2 * T + 16, T), BF16)], [SMEM, VMEM, VMEM])(
        meta, got, grads
    )
    got = exchange(send, "z")
    grad_features, half, grad_bias = call(
        last_kernel,
        [((T, T), F32), ((T, T), F32), ((1, 2 * T), F32)],
        [VMEM, VMEM],
    )(got, scale)
    other = swap(half, "core")
    grad_weight = jnp.concatenate(
        [jnp.where(even, half, other), jnp.where(even, other, half)], axis=1
    )
    return act, grad_weight, grad_bias[0], grad_features


def solution(mesh):
    fine = Mesh(mesh.devices.reshape(Z, YL, CORE, X, YH), BLK + REP)
    return jax.shard_map(
        on_device,
        mesh=fine,
        in_specs=(
            P(BLK, None),
            P(BLK),
            P(BLK, REP, None),
            P(BLK, REP),
            P(BLK, REP, None, None, None),
            P(),
            P(),
            P(BLK + REP, None),
        ),
        out_specs=(P(BLK + REP, None), P(), P(), P(BLK + REP, None)),
        check_vma=False,
    )
```

```python
import functools

import jax
import jax.numpy as jnp
from jax import lax
from jax.experimental import pallas as pl
from jax.experimental.pallas import tpu as pltpu
from jax.sharding import Mesh
from jax.sharding import PartitionSpec as P

Z, YL, CORE, X, YH = 8, 2, 2, 4, 2
BLK = ("z", "yl", "core")
REP = ("x", "yh")
T = 128
ROWS = 8
STEPS = 4
SLOTS = 6
HALF = ROWS // 2
GRAD = 48
F32 = jnp.float32
BF16 = jnp.bfloat16

VMEM = pl.BlockSpec(memory_space=pltpu.VMEM)
SMEM = pl.BlockSpec(memory_space=pltpu.SMEM)
HBM = pl.BlockSpec(memory_space=pltpu.HBM)
PARAMS = pltpu.CompilerParams(vmem_limit_bytes=32 * 1024 * 1024)


def bias_rows(total):
    high = total.astype(BF16)
    low = (total - high.astype(F32)).astype(BF16)
    return jnp.concatenate([high, low, jnp.zeros((12, T), BF16)], axis=0)


def prologue_kernel(rep, features, degrees, low, high, scale):
    rows = jnp.concatenate([degrees[...].astype(F32), jnp.ones((T - ROWS, T), F32)], axis=0)
    columns = lax.rsqrt(rows.T)
    for j in range(ROWS):
        inv_root = jnp.broadcast_to(columns[:, j : j + 1], (T, T))
        tile = (features[j * T : (j + 1) * T].astype(F32) * inv_root).astype(BF16)
        half = low if j < HALF else high
        half[j % HALF] = tile

        @pl.when(rep[0] == j)
        def _():
            scale[...] = inv_root


def tile_of(low, high):
    def tile_at(col):
        at = lax.rem(col, HALF)
        return jnp.where(col < HALF, low[at], high[at])

    return tile_at


def product(meta, edges, i, s, tile_at):
    picked = []
    for c in range(SLOTS):
        tile = tile_at(meta[c, s, i])
        picked.append(jnp.where(c < meta[6, s, i], tile, jnp.zeros_like(tile)))
    left = jnp.concatenate([edges[i, s, c] for c in range(SLOTS)], axis=1)
    return jnp.dot(left, jnp.concatenate(picked, axis=0), preferred_element_type=F32)


def first_kernel(meta, edges, low, high, held, out, sems):
    copies = [pltpu.make_async_copy(edges.at[i], held.at[i], sems.at[i]) for i in range(ROWS)]
    for copy in copies:
        copy.start()
    for i in range(ROWS):
        copies[i].wait()
        out[i] = product(meta, held, i, 0, tile_of(low, high))


def second_kernel(meta, held, far_low, far_high, near_low, near_high, total, out):
    step = 3 - 2 * meta[7, 0, 0]
    for i in range(ROWS):
        out[i] = (
            total[i]
            + product(meta, held, i, 2, tile_of(far_low, far_high))
            + product(meta, held, i, step, tile_of(near_low, near_high))
        )


def third_kernel(meta, held, low, high, total, out):
    step = 1 + 2 * meta[7, 0, 0]
    for i in range(ROWS):
        out[i] = (total[i] + product(meta, held, i, step, tile_of(low, high))).astype(BF16)


def dense_kernel(parts, scale, weight, bias, cot, act, send):
    total = parts[0].astype(F32)
    for j in range(1, ROWS):
        total += parts[j].astype(F32)
    agg = (scale[...] * total).astype(BF16)
    pre = jnp.dot(agg, weight[...], preferred_element_type=F32) + bias[...]
    sigma = jax.nn.sigmoid(pre)
    act[...] = (pre * sigma).astype(BF16)
    grad_pre = cot[...].astype(F32) * sigma * (1.0 + pre * (1.0 - sigma))
    half = grad_pre.astype(BF16)
    grad_w = lax.dot_general(agg, half, (((0,), (0,)), ((), ())), preferred_element_type=F32)
    grad_b = jnp.sum(grad_pre, axis=0, keepdims=True)
    grad_b = jnp.concatenate([grad_b[:, :T], grad_b[:, T:]], axis=0)
    back = lax.dot_general(
        half, weight[...], (((1,), (1,)), ((), ())), preferred_element_type=F32
    )
    back = (scale[...] * back).astype(BF16)
    rows_b = bias_rows(grad_b)
    grad_w = grad_w.astype(BF16)
    for j in range(ROWS):
        send[j, 0:T] = back
        send[j, T : T + 16] = grad_w[16 * j : 16 * j + 16, :T]
        send[j, T + 16 : T + 32] = grad_w[16 * j : 16 * j + 16, T:]
        send[j, T + 32 : T + 48] = rows_b


def column_sums(meta, held, got, s, sums):
    sums[...] = jnp.zeros_like(sums)
    for i in range(ROWS):
        back = got[i, 0:T].T
        right = jnp.concatenate([held[i, s, c] for c in range(SLOTS)], axis=1)
        prod = jnp.dot(back, right, preferred_element_type=F32)
        for c in range(SLOTS):
            part = prod[:, c * T : (c + 1) * T]
            at = meta[c, s, i]
            sums[at] += jnp.where(c < meta[6, s, i], part, jnp.zeros_like(part))


def near_sums_kernel(meta, held, got, near0, near1, grads, sums):
    total = got[0, T:].astype(F32)
    for j in range(1, ROWS):
        total += got[j, T:].astype(F32)
    grads[0:32] = total[0:32]
    grads[32:40] = jnp.concatenate(
        [total[32:34] + total[34:36], jnp.zeros((6, T), F32)], axis=0
    )
    column_sums(meta, held, got, 1 + 2 * meta[7, 0, 0], sums)
    near1[...] = sums[...].astype(BF16)
    column_sums(meta, held, got, 3 - 2 * meta[7, 0, 0], sums)
    near0[...] = sums[...].astype(BF16)


def far_sums_kernel(meta, held, got, far, sums):
    column_sums(meta, held, got, 2, sums)
    far[...] = sums[...].astype(BF16)


def own_sums_kernel(meta, held, got, out, sums):
    column_sums(meta, held, got, 0, sums)
    out[...] = sums[...]


def near_kernel(far, near, low, high):
    low[...] = (far[0:HALF].astype(F32) + near[0:HALF].astype(F32)).astype(BF16)
    high[...] = (far[HALF:].astype(F32) + near[HALF:].astype(F32)).astype(BF16)


def half_kernel(first, own, near, far, out):
    rows = pl.ds(first, HALF)
    total = own[rows] + near[rows].astype(F32) + far[...].astype(F32)
    out[...] = total.astype(BF16)


def gather_kernel(low, high, grads, out):
    mine = grads[0:32].astype(BF16)
    for j in range(ROWS):
        out[j, 0:T] = low[j] if j < HALF else high[j - HALF]
        out[j, T:] = mine


def last_kernel(got, scale, grads, grad_features, grad_weight, grad_bias):
    total = got[0, 0:T].astype(F32)
    for j in range(1, ROWS):
        total += got[j, 0:T].astype(F32)
    grad_features[...] = scale[...] * total.T
    for j in range(ROWS):
        rows = slice(16 * j, 16 * j + 16)
        grad_weight[rows, :T] = got[j, T : T + 16].astype(F32)
        grad_weight[rows, T:] = got[j, T + 16 :].astype(F32)
    grad_bias[...] = jnp.concatenate([grads[32:33], grads[33:34]], axis=1)


def call(kernel, out, in_specs, scratch=(), flops=0, moved=1 << 20):
    return pl.pallas_call(
        kernel,
        out_shape=[jax.ShapeDtypeStruct(*o) for o in out],
        in_specs=in_specs,
        out_specs=[VMEM] * len(out),
        scratch_shapes=list(scratch),
        cost_estimate=pl.CostEstimate(flops=flops, bytes_accessed=moved, transcendentals=0),
        compiler_params=PARAMS,
    )


def pinned(value):
    return pltpu.with_memory_space_constraint(value, pltpu.HBM)


def exchange(value, axes):
    return lax.all_to_all(value, axes, 0, 0, tiled=True)


def move(value, to):
    blk, rep = Z * YL * CORE, X * YH
    pairs = []
    for b in range(blk):
        for r in range(rep):
            to_b, to_r = to(b, r)
            pairs.append((b * rep + r, to_b % blk * rep + to_r))
    return lax.ppermute(value, BLK + REP, pairs)


def swap(value, bit):
    return move(value, lambda b, r: (b ^ bit, r))


def on_device(features, degrees, cols, counts, edges, weight, bias, cot):
    z, yl, core = (lax.axis_index(a) for a in BLK)
    rep = lax.axis_index(REP)
    place = lax.broadcasted_iota(jnp.int32, (1, STEPS, ROWS), 2)
    place = jnp.where(place == 0, core, 0)
    meta = jnp.concatenate([cols.transpose(2, 1, 0), counts.T[None], place], axis=0)

    tiles, half = (ROWS, T, T), (HALF, T, T)
    low, high, scale = call(
        prologue_kernel,
        [(half, BF16), (half, BF16), ((T, T), F32)],
        [SMEM, VMEM, VMEM],
    )(rep.astype(jnp.int32)[None], pinned(features), pinned(degrees.reshape(ROWS, T)))

    low = move(low, lambda b, r: (b + 4 * r, r))
    high = move(high, lambda b, r: (b + 4 * (r ^ 2), r ^ 2))
    far_low, far_high = (move(v, lambda b, r: (b + 2, r)) for v in (low, high))
    near_low, near_high = (move(v, lambda b, r: (b + 1 + 2 * (b % 2), r)) for v in (low, high))

    work = 2 * ROWS * SLOTS * T * T * T
    held, total = call(
        first_kernel,
        [(edges.shape, BF16), (tiles, F32)],
        [SMEM, HBM, VMEM, VMEM],
        [pltpu.SemaphoreType.DMA((ROWS,))],
        work,
        8 << 20,
    )(meta, pinned(edges), low, high)
    far_low, far_high, total = lax.optimization_barrier((far_low, far_high, total))
    last_low, last_high = swap(far_low, 1), swap(far_high, 1)
    (total,) = call(second_kernel, [(tiles, F32)], [SMEM] + [VMEM] * 6, (), 2 * work, 6 << 20)(
        meta, held, far_low, far_high, near_low, near_high, total
    )
    (parts,) = call(third_kernel, [(tiles, BF16)], [SMEM] + [VMEM] * 4, (), work, 3 << 20)(
        meta, held, last_low, last_high, total
    )
    parts = exchange(parts, REP)

    act, send = call(
        dense_kernel,
        [(cot.shape, BF16), ((ROWS, T + GRAD, T), BF16)],
        [VMEM] * 5,
    )(parts, scale, weight, bias[None], cot)
    got = exchange(send, REP)

    sums = [pltpu.VMEM(tiles, F32)]
    near, last, grads = call(
        near_sums_kernel,
        [(tiles, BF16), (tiles, BF16), ((40, T), F32)],
        [SMEM, VMEM, VMEM],
        sums,
        2 * work,
        6 << 20,
    )(meta, held, got)
    last = swap(last, 1)
    near = move(near, lambda b, r: (b - 3 + 2 * (b % 2), r))
    (far,) = call(far_sums_kernel, [(tiles, BF16)], [SMEM, VMEM, VMEM], sums, work, 3 << 20)(
        meta, held, got
    )
    far_low, far_high = call(near_kernel, [(half, BF16), (half, BF16)], [VMEM] * 2)(far, last)
    far_low, far_high, got, grads = lax.optimization_barrier((far_low, far_high, got, grads))
    far_low, far_high = (move(v, lambda b, r: (b - 2, r)) for v in (far_low, far_high))
    (own,) = call(own_sums_kernel, [(tiles, F32)], [SMEM] + [VMEM] * 2, sums, work, 3 << 20)(
        meta, held, got
    )
    grads = grads + swap(grads, 16)
    own, grads = lax.optimization_barrier((own, grads))
    low, high = (
        call(functools.partial(half_kernel, first), [(half, BF16)], [VMEM] * 3)(own, near, far)[0]
        for first, far in ((0, far_low), (HALF, far_high))
    )
    low = move(low, lambda b, r: (b - 4 * r, r))
    high = move(high, lambda b, r: (b - 4 * r, r ^ 2))
    for bit in (8, 4, 2, 1):
        grads = grads + swap(grads, bit)
    (send,) = call(gather_kernel, [((ROWS, T + 32, T), BF16)], [VMEM] * 3)(low, high, grads)
    got = exchange(send, REP)
    grad_features, grad_weight, grad_bias = call(
        last_kernel,
        [((T, T), F32), ((T, 2 * T), F32), ((1, 2 * T), F32)],
        [VMEM] * 3,
    )(got, scale, grads)
    return act, grad_weight, grad_bias[0], grad_features


def solution(mesh):
    fine = Mesh(mesh.devices.reshape(Z, YL, CORE, X, YH), BLK + REP)
    return jax.shard_map(
        on_device,
        mesh=fine,
        in_specs=(
            P(BLK, None),
            P(BLK),
            P(BLK, REP, None),
            P(BLK, REP),
            P(BLK, REP, None, None, None),
            P(),
            P(),
            P(BLK + REP, None),
        ),
        out_specs=(P(BLK + REP, None), P(), P(), P(BLK + REP, None)),
        check_vma=False,
    )
```

```python
import functools

import jax
import jax.numpy as jnp
from jax import lax
from jax.experimental import pallas as pl
from jax.experimental.pallas import tpu as pltpu
from jax.sharding import Mesh
from jax.sharding import PartitionSpec as P

Z, YL, CORE, X, YH = 8, 2, 2, 4, 2
BLK = ("z", "yl", "core")
REP = ("x", "yh")
T = 128
ROWS = 8
STEPS = 4
SLOTS = 6
HALF = ROWS // 2
GRAD = 48
F32 = jnp.float32
BF16 = jnp.bfloat16

VMEM = pl.BlockSpec(memory_space=pltpu.VMEM)
SMEM = pl.BlockSpec(memory_space=pltpu.SMEM)
HBM = pl.BlockSpec(memory_space=pltpu.HBM)
PARAMS = pltpu.CompilerParams(vmem_limit_bytes=32 * 1024 * 1024)


def bias_rows(total):
    high = total.astype(BF16)
    low = (total - high.astype(F32)).astype(BF16)
    return jnp.concatenate([high, low, jnp.zeros((12, T), BF16)], axis=0)


def prologue_kernel(rep, features, degrees, low, high, scale):
    rows = jnp.concatenate([degrees[...].astype(F32), jnp.ones((T - ROWS, T), F32)], axis=0)
    columns = lax.rsqrt(rows.T)
    for j in range(ROWS):
        inv_root = jnp.broadcast_to(columns[:, j : j + 1], (T, T))
        tile = (features[j * T : (j + 1) * T].astype(F32) * inv_root).astype(BF16)
        half = low if j < HALF else high
        half[j % HALF] = tile

        @pl.when(rep[0] == j)
        def _():
            scale[...] = inv_root


def tile_of(low, high):
    def tile_at(col):
        at = lax.rem(col, HALF)
        return jnp.where(col < HALF, low[at], high[at])

    return tile_at


def product(meta, edges, i, s, tile_at):
    picked = []
    for c in range(SLOTS):
        tile = tile_at(meta[c, s, i])
        picked.append(jnp.where(c < meta[6, s, i], tile, jnp.zeros_like(tile)))
    left = jnp.concatenate([edges[i, s, c] for c in range(SLOTS)], axis=1)
    return jnp.dot(left, jnp.concatenate(picked, axis=0), preferred_element_type=F32)


def load_kernel(edges, held, sem):
    copy = pltpu.make_async_copy(edges, held, sem)
    copy.start()
    copy.wait()


def first_kernel(meta, held, low, high, out):
    for i in range(ROWS):
        out[i] = product(meta, held, i, 0, tile_of(low, high))


def second_kernel(meta, held, low, high, total, out):
    for i in range(ROWS):
        out[i] = total[i] + product(meta, held, i, 2, tile_of(low, high))


def third_kernel(meta, held, near_low, near_high, last_low, last_high, total, out):
    odd = meta[7, 0, 0]
    for i in range(ROWS):
        out[i] = (
            total[i]
            + product(meta, held, i, 3 - 2 * odd, tile_of(near_low, near_high))
            + product(meta, held, i, 1 + 2 * odd, tile_of(last_low, last_high))
        ).astype(BF16)


def dense_kernel(parts, scale, weight, bias, cot, act, send):
    total = parts[0].astype(F32)
    for j in range(1, ROWS):
        total += parts[j].astype(F32)
    agg = (scale[...] * total).astype(BF16)
    pre = jnp.dot(agg, weight[...], preferred_element_type=F32) + bias[...]
    sigma = jax.nn.sigmoid(pre)
    act[...] = (pre * sigma).astype(BF16)
    grad_pre = cot[...].astype(F32) * sigma * (1.0 + pre * (1.0 - sigma))
    half = grad_pre.astype(BF16)
    grad_w = lax.dot_general(agg, half, (((0,), (0,)), ((), ())), preferred_element_type=F32)
    grad_b = jnp.sum(grad_pre, axis=0, keepdims=True)
    grad_b = jnp.concatenate([grad_b[:, :T], grad_b[:, T:]], axis=0)
    back = lax.dot_general(
        half, weight[...], (((1,), (1,)), ((), ())), preferred_element_type=F32
    )
    back = (scale[...] * back).astype(BF16)
    rows_b = bias_rows(grad_b)
    grad_w = grad_w.astype(BF16)
    for j in range(ROWS):
        send[j, 0:T] = back
        send[j, T : T + 16] = grad_w[16 * j : 16 * j + 16, :T]
        send[j, T + 16 : T + 32] = grad_w[16 * j : 16 * j + 16, T:]
        send[j, T + 32 : T + 48] = rows_b


def column_sums(meta, held, got, s, sums):
    sums[...] = jnp.zeros_like(sums)
    for i in range(ROWS):
        back = got[i, 0:T].T
        right = jnp.concatenate([held[i, s, c] for c in range(SLOTS)], axis=1)
        prod = jnp.dot(back, right, preferred_element_type=F32)
        for c in range(SLOTS):
            part = prod[:, c * T : (c + 1) * T]
            at = meta[c, s, i]
            sums[at] += jnp.where(c < meta[6, s, i], part, jnp.zeros_like(part))


def near_sums_kernel(meta, held, got, near0, near1, grads, sums):
    total = got[0, T:].astype(F32)
    for j in range(1, ROWS):
        total += got[j, T:].astype(F32)
    grads[0:32] = total[0:32]
    grads[32:40] = jnp.concatenate(
        [total[32:34] + total[34:36], jnp.zeros((6, T), F32)], axis=0
    )
    column_sums(meta, held, got, 1 + 2 * meta[7, 0, 0], sums)
    near1[...] = sums[...].astype(BF16)
    column_sums(meta, held, got, 3 - 2 * meta[7, 0, 0], sums)
    near0[...] = sums[...].astype(BF16)


def far_sums_kernel(meta, held, got, far, sums):
    column_sums(meta, held, got, 2, sums)
    far[...] = sums[...].astype(BF16)


def own_sums_kernel(meta, held, got, out, sums):
    column_sums(meta, held, got, 0, sums)
    out[...] = sums[...]


def near_kernel(far, near, low, high):
    low[...] = (far[0:HALF].astype(F32) + near[0:HALF].astype(F32)).astype(BF16)
    high[...] = (far[HALF:].astype(F32) + near[HALF:].astype(F32)).astype(BF16)


def half_kernel(first, own, near, far, out):
    rows = pl.ds(first, HALF)
    total = own[rows] + near[rows].astype(F32) + far[...].astype(F32)
    out[...] = total.astype(BF16)


def gather_kernel(low, high, grads, out):
    mine = grads[0:32].astype(BF16)
    for j in range(ROWS):
        out[j, 0:T] = low[j] if j < HALF else high[j - HALF]
        out[j, T:] = mine


def last_kernel(got, scale, grads, grad_features, grad_weight, grad_bias):
    total = got[0, 0:T].astype(F32)
    for j in range(1, ROWS):
        total += got[j, 0:T].astype(F32)
    grad_features[...] = scale[...] * total.T
    for j in range(ROWS):
        rows = slice(16 * j, 16 * j + 16)
        grad_weight[rows, :T] = got[j, T : T + 16].astype(F32)
        grad_weight[rows, T:] = got[j, T + 16 :].astype(F32)
    grad_bias[...] = jnp.concatenate([grads[32:33], grads[33:34]], axis=1)


def call(kernel, out, in_specs, scratch=(), flops=0, moved=1 << 20):
    return pl.pallas_call(
        kernel,
        out_shape=[jax.ShapeDtypeStruct(*o) for o in out],
        in_specs=in_specs,
        out_specs=[VMEM] * len(out),
        scratch_shapes=list(scratch),
        cost_estimate=pl.CostEstimate(flops=flops, bytes_accessed=moved, transcendentals=0),
        compiler_params=PARAMS,
    )


def pinned(value):
    return pltpu.with_memory_space_constraint(value, pltpu.HBM)


def exchange(value, axes):
    return lax.all_to_all(value, axes, 0, 0, tiled=True)


def move(value, to):
    blk, rep = Z * YL * CORE, X * YH
    pairs = []
    for b in range(blk):
        for r in range(rep):
            to_b, to_r = to(b, r)
            pairs.append((b * rep + r, to_b % blk * rep + to_r))
    return lax.ppermute(value, BLK + REP, pairs)


def swap(value, bit):
    return move(value, lambda b, r: (b ^ bit, r))


def on_device(features, degrees, cols, counts, edges, weight, bias, cot):
    z, yl, core = (lax.axis_index(a) for a in BLK)
    rep = lax.axis_index(REP)
    place = lax.broadcasted_iota(jnp.int32, (1, STEPS, ROWS), 2)
    place = jnp.where(place == 0, core, 0)
    meta = jnp.concatenate([cols.transpose(2, 1, 0), counts.T[None], place], axis=0)

    tiles, half = (ROWS, T, T), (HALF, T, T)
    low, high, scale = call(
        prologue_kernel,
        [(half, BF16), (half, BF16), ((T, T), F32)],
        [SMEM, VMEM, VMEM],
    )(rep.astype(jnp.int32)[None], pinned(features), pinned(degrees.reshape(ROWS, T)))

    low = move(low, lambda b, r: (b + 4 * r, r))
    high = move(high, lambda b, r: (b + 4 * (r ^ 2), r ^ 2))
    (held,) = call(
        load_kernel, [(edges.shape, BF16)], [HBM], [pltpu.SemaphoreType.DMA], 0, 12 << 20
    )(pinned(edges))
    low, high, held, meta = lax.optimization_barrier((low, high, held, meta))
    far_low, far_high = (move(v, lambda b, r: (b + 2, r)) for v in (low, high))

    work = 2 * ROWS * SLOTS * T * T * T
    (total,) = call(first_kernel, [(tiles, F32)], [SMEM] + [VMEM] * 3, (), work, 3 << 20)(
        meta, held, low, high
    )
    low, high, total = lax.optimization_barrier((low, high, total))
    near_low, near_high = (move(v, lambda b, r: (b + 1 + 2 * (b % 2), r)) for v in (low, high))
    last_low, last_high = swap(far_low, 1), swap(far_high, 1)
    (total,) = call(second_kernel, [(tiles, F32)], [SMEM] + [VMEM] * 4, (), work, 3 << 20)(
        meta, held, far_low, far_high, total
    )
    (parts,) = call(third_kernel, [(tiles, BF16)], [SMEM] + [VMEM] * 6, (), 2 * work, 6 << 20)(
        meta, held, near_low, near_high, last_low, last_high, total
    )
    parts = exchange(parts, REP)

    act, send = call(
        dense_kernel,
        [(cot.shape, BF16), ((ROWS, T + GRAD, T), BF16)],
        [VMEM] * 5,
    )(parts, scale, weight, bias[None], cot)
    got = exchange(send, REP)

    sums = [pltpu.VMEM(tiles, F32)]
    near, last, grads = call(
        near_sums_kernel,
        [(tiles, BF16), (tiles, BF16), ((40, T), F32)],
        [SMEM, VMEM, VMEM],
        sums,
        2 * work,
        6 << 20,
    )(meta, held, got)
    last = swap(last, 1)
    near = move(near, lambda b, r: (b - 3 + 2 * (b % 2), r))
    (far,) = call(far_sums_kernel, [(tiles, BF16)], [SMEM, VMEM, VMEM], sums, work, 3 << 20)(
        meta, held, got
    )
    far_low, far_high = call(near_kernel, [(half, BF16), (half, BF16)], [VMEM] * 2)(far, last)
    grads = grads + swap(grads, 4)
    far_low, far_high, got, grads = lax.optimization_barrier((far_low, far_high, got, grads))
    far_low, far_high = (move(v, lambda b, r: (b - 2, r)) for v in (far_low, far_high))
    (own,) = call(own_sums_kernel, [(tiles, F32)], [SMEM] + [VMEM] * 2, sums, work, 3 << 20)(
        meta, held, got
    )
    grads = grads + swap(grads, 8)
    own, grads = lax.optimization_barrier((own, grads))
    low, high = (
        call(functools.partial(half_kernel, first), [(half, BF16)], [VMEM] * 3)(own, near, far)[0]
        for first, far in ((0, far_low), (HALF, far_high))
    )
    low = move(low, lambda b, r: (b - 4 * r, r))
    high = move(high, lambda b, r: (b - 4 * r, r ^ 2))
    for bit in (2, 1, 16):
        grads = grads + swap(grads, bit)
    (send,) = call(gather_kernel, [((ROWS, T + 32, T), BF16)], [VMEM] * 3)(low, high, grads)
    got = exchange(send, REP)
    grad_features, grad_weight, grad_bias = call(
        last_kernel,
        [((T, T), F32), ((T, 2 * T), F32), ((1, 2 * T), F32)],
        [VMEM] * 3,
    )(got, scale, grads)
    return act, grad_weight, grad_bias[0], grad_features


def solution(mesh):
    fine = Mesh(mesh.devices.reshape(Z, YL, CORE, X, YH), BLK + REP)
    return jax.shard_map(
        on_device,
        mesh=fine,
        in_specs=(
            P(BLK, None),
            P(BLK),
            P(BLK, REP, None),
            P(BLK, REP),
            P(BLK, REP, None, None, None),
            P(),
            P(),
            P(BLK + REP, None),
        ),
        out_specs=(P(BLK + REP, None), P(), P(), P(BLK + REP, None)),
        check_vma=False,
    )
```

```python
import functools

import jax
import jax.numpy as jnp
from jax import lax
from jax.experimental import pallas as pl
from jax.experimental.pallas import tpu as pltpu
from jax.sharding import Mesh
from jax.sharding import PartitionSpec as P

Z, YL, CORE, X, YH = 8, 2, 2, 4, 2
BLK = ("z", "yl", "core")
REP = ("x", "yh")
T = 128
ROWS = 8
STEPS = 4
SLOTS = 6
HALF = ROWS // 2
NODES = ROWS * T
GRAD = 48
F32 = jnp.float32
BF16 = jnp.bfloat16

VMEM = pl.BlockSpec(memory_space=pltpu.VMEM)
SMEM = pl.BlockSpec(memory_space=pltpu.SMEM)
HBM = pl.BlockSpec(memory_space=pltpu.HBM)
PARAMS = pltpu.CompilerParams(vmem_limit_bytes=32 * 1024 * 1024)


def bias_rows(total):
    high = total.astype(BF16)
    low = (total - high.astype(F32)).astype(BF16)
    return jnp.concatenate([high, low, jnp.zeros((12, T), BF16)], axis=0)


def prologue_kernel(rep, features, degrees, low, high, scale):
    rows = jnp.concatenate([degrees[...].astype(F32), jnp.ones((T - ROWS, T), F32)], axis=0)
    columns = lax.rsqrt(rows.T)
    for j in range(ROWS):
        inv_root = jnp.broadcast_to(columns[:, j : j + 1], (T, T))
        tile = (features[j * T : (j + 1) * T].astype(F32) * inv_root).astype(BF16)
        half = low if j < HALF else high
        half[j % HALF] = tile

        @pl.when(rep[0] == j)
        def _():
            scale[...] = inv_root


def tile_of(low, high):
    def tile_at(col):
        at = lax.rem(col, HALF)
        return jnp.where(col < HALF, low[at], high[at])

    return tile_at


def product(meta, edges, i, s, tile_at):
    picked = []
    for c in range(SLOTS):
        tile = tile_at(meta[c, s, i])
        picked.append(jnp.where(c < meta[6, s, i], tile, jnp.zeros_like(tile)))
    left = jnp.concatenate([edges[i, s, c] for c in range(SLOTS)], axis=1)
    return jnp.dot(left, jnp.concatenate(picked, axis=0), preferred_element_type=F32)


def load_kernel(edges, held, sem):
    copy = pltpu.make_async_copy(edges, held, sem)
    copy.start()
    copy.wait()


def first_kernel(meta, held, low, high, out):
    for i in range(ROWS):
        out[i] = product(meta, held, i, 0, tile_of(low, high))


def second_kernel(meta, held, low, high, total, out):
    for i in range(ROWS):
        out[i] = total[i] + product(meta, held, i, 2, tile_of(low, high))


def third_kernel(meta, held, near_low, near_high, last_low, last_high, total, out):
    odd = meta[7, 0, 0]
    for i in range(ROWS):
        out[i] = (
            total[i]
            + product(meta, held, i, 3 - 2 * odd, tile_of(near_low, near_high))
            + product(meta, held, i, 1 + 2 * odd, tile_of(last_low, last_high))
        ).astype(BF16)


def dense_kernel(parts, scale, weight, bias, cot, act, send):
    total = parts[0].astype(F32)
    for j in range(1, ROWS):
        total += parts[j].astype(F32)
    agg = (scale[...] * total).astype(BF16)
    pre = jnp.dot(agg, weight[...], preferred_element_type=F32) + bias[...]
    sigma = jax.nn.sigmoid(pre)
    act[...] = (pre * sigma).astype(BF16)
    grad_pre = cot[...].astype(F32) * sigma * (1.0 + pre * (1.0 - sigma))
    half = grad_pre.astype(BF16)
    grad_w = lax.dot_general(agg, half, (((0,), (0,)), ((), ())), preferred_element_type=F32)
    grad_b = jnp.sum(grad_pre, axis=0, keepdims=True)
    grad_b = jnp.concatenate([grad_b[:, :T], grad_b[:, T:]], axis=0)
    back = lax.dot_general(
        half, weight[...], (((1,), (1,)), ((), ())), preferred_element_type=F32
    )
    back = (scale[...] * back).astype(BF16)
    rows_b = bias_rows(grad_b)
    grad_w = grad_w.astype(BF16)
    for j in range(ROWS):
        send[j, 0:T] = back
        send[j, T : T + 16] = grad_w[16 * j : 16 * j + 16, :T]
        send[j, T + 16 : T + 32] = grad_w[16 * j : 16 * j + 16, T:]
        send[j, T + 32 : T + 48] = rows_b


def column_sums(meta, held, got, s, sums):
    sums[...] = jnp.zeros_like(sums)
    for i in range(ROWS):
        back = got[i, 0:T].T
        right = jnp.concatenate([held[i, s, c] for c in range(SLOTS)], axis=1)
        prod = jnp.dot(back, right, preferred_element_type=F32)
        for c in range(SLOTS):
            part = prod[:, c * T : (c + 1) * T]
            at = meta[c, s, i]
            sums[at] += jnp.where(c < meta[6, s, i], part, jnp.zeros_like(part))


def near_sums_kernel(meta, held, got, near, last, sums):
    total = got[0, T:].astype(F32)
    for j in range(1, ROWS):
        total += got[j, T:].astype(F32)
    total = jnp.concatenate(
        [total[0:32], total[32:34] + total[34:36], jnp.zeros((14, T), F32)], axis=0
    )
    high = total.astype(BF16)
    last[NODES : NODES + GRAD] = high
    last[NODES + GRAD :] = (total - high.astype(F32)).astype(BF16)
    column_sums(meta, held, got, 1 + 2 * meta[7, 0, 0], sums)
    last[0:NODES] = sums[...].astype(BF16).reshape(NODES, T)
    column_sums(meta, held, got, 3 - 2 * meta[7, 0, 0], sums)
    near[...] = sums[...].astype(BF16)


def far_sums_kernel(meta, held, got, far, sums):
    column_sums(meta, held, got, 2, sums)
    far[...] = sums[...].astype(BF16)


def own_sums_kernel(meta, held, got, out, sums):
    column_sums(meta, held, got, 0, sums)
    out[...] = sums[...]


def grads_of(rows):
    return rows[NODES : NODES + GRAD].astype(F32) + rows[NODES + GRAD :].astype(F32)


def near_kernel(far, mine, other, low, high, grads):
    for j in range(ROWS):
        half = low if j < HALF else high
        rows = other[j * T : (j + 1) * T].astype(F32)
        half[j % HALF] = (far[j].astype(F32) + rows).astype(BF16)
    grads[...] = grads_of(mine) + grads_of(other)


def half_kernel(first, own, near, far, out):
    rows = pl.ds(first, HALF)
    total = own[rows] + near[rows].astype(F32) + far[...].astype(F32)
    out[...] = total.astype(BF16)


def gather_kernel(low, high, planes, out, grads):
    total = planes[0]
    for p in range(1, Z):
        total += planes[p]
    grads[...] = total
    mine = total[0:32].astype(BF16)
    for j in range(ROWS):
        out[j, 0:T] = low[j] if j < HALF else high[j - HALF]
        out[j, T:] = mine


def last_kernel(got, scale, grads, grad_features, grad_weight, grad_bias):
    total = got[0, 0:T].astype(F32)
    for j in range(1, ROWS):
        total += got[j, 0:T].astype(F32)
    grad_features[...] = scale[...] * total.T
    for j in range(ROWS):
        rows = slice(16 * j, 16 * j + 16)
        grad_weight[rows, :T] = got[j, T : T + 16].astype(F32)
        grad_weight[rows, T:] = got[j, T + 16 :].astype(F32)
    grad_bias[...] = jnp.concatenate([grads[32:33], grads[33:34]], axis=1)


def call(kernel, out, in_specs, scratch=(), flops=0, moved=1 << 20):
    return pl.pallas_call(
        kernel,
        out_shape=[jax.ShapeDtypeStruct(*o) for o in out],
        in_specs=in_specs,
        out_specs=[VMEM] * len(out),
        scratch_shapes=list(scratch),
        cost_estimate=pl.CostEstimate(flops=flops, bytes_accessed=moved, transcendentals=0),
        compiler_params=PARAMS,
    )


def pinned(value):
    return pltpu.with_memory_space_constraint(value, pltpu.HBM)


def exchange(value, axes):
    return lax.all_to_all(value, axes, 0, 0, tiled=True)


def move(value, to):
    blk, rep = Z * YL * CORE, X * YH
    pairs = []
    for b in range(blk):
        for r in range(rep):
            to_b, to_r = to(b, r)
            pairs.append((b * rep + r, to_b % blk * rep + to_r))
    return lax.ppermute(value, BLK + REP, pairs)


def swap(value, bit):
    return move(value, lambda b, r: (b ^ bit, r))


def on_device(features, degrees, cols, counts, edges, weight, bias, cot):
    z, yl, core = (lax.axis_index(a) for a in BLK)
    rep = lax.axis_index(REP)
    place = lax.broadcasted_iota(jnp.int32, (1, STEPS, ROWS), 2)
    place = jnp.where(place == 0, core, 0)
    meta = jnp.concatenate([cols.transpose(2, 1, 0), counts.T[None], place], axis=0)

    tiles, half = (ROWS, T, T), (HALF, T, T)
    low, high, scale = call(
        prologue_kernel,
        [(half, BF16), (half, BF16), ((T, T), F32)],
        [SMEM, VMEM, VMEM],
    )(rep.astype(jnp.int32)[None], pinned(features), pinned(degrees.reshape(ROWS, T)))

    low = move(low, lambda b, r: (b + 4 * r, r))
    high = move(high, lambda b, r: (b + 4 * (r ^ 2), r ^ 2))
    (held,) = call(
        load_kernel, [(edges.shape, BF16)], [HBM], [pltpu.SemaphoreType.DMA], 0, 12 << 20
    )(pinned(edges))
    low, held, meta = lax.optimization_barrier((low, held, meta))
    far_low, far_high = (move(v, lambda b, r: (b + 2, r)) for v in (low, high))
    near_low = move(low, lambda b, r: (b + 1 + 2 * (b % 2), r))

    work = 2 * ROWS * SLOTS * T * T * T
    (total,) = call(first_kernel, [(tiles, F32)], [SMEM] + [VMEM] * 3, (), work, 3 << 20)(
        meta, held, low, high
    )
    high, total = lax.optimization_barrier((high, total))
    near_high = move(high, lambda b, r: (b + 1 + 2 * (b % 2), r))
    last_low, last_high = swap(far_low, 1), swap(far_high, 1)
    (total,) = call(second_kernel, [(tiles, F32)], [SMEM] + [VMEM] * 4, (), work, 3 << 20)(
        meta, held, far_low, far_high, total
    )
    (parts,) = call(third_kernel, [(tiles, BF16)], [SMEM] + [VMEM] * 6, (), 2 * work, 6 << 20)(
        meta, held, near_low, near_high, last_low, last_high, total
    )
    parts = exchange(parts, REP)

    act, send = call(
        dense_kernel,
        [(cot.shape, BF16), ((ROWS, T + GRAD, T), BF16)],
        [VMEM] * 5,
    )(parts, scale, weight, bias[None], cot)
    got = exchange(send, REP)

    sums = [pltpu.VMEM(tiles, F32)]
    near, mine = call(
        near_sums_kernel,
        [(tiles, BF16), ((NODES + 2 * GRAD, T), BF16)],
        [SMEM, VMEM, VMEM],
        sums,
        2 * work,
        6 << 20,
    )(meta, held, got)
    other = swap(mine, 1)
    near = move(near, lambda b, r: (b - 3 + 2 * (b % 2), r))
    (far,) = call(far_sums_kernel, [(tiles, BF16)], [SMEM, VMEM, VMEM], sums, work, 3 << 20)(
        meta, held, got
    )
    far_low, far_high, grads = call(
        near_kernel, [(half, BF16), (half, BF16), ((GRAD, T), F32)], [VMEM] * 3
    )(far, mine, other)
    far_low, far_high, got, grads = lax.optimization_barrier((far_low, far_high, got, grads))
    far_low, far_high = (move(v, lambda b, r: (b - 2, r)) for v in (far_low, far_high))
    (own,) = call(own_sums_kernel, [(tiles, F32)], [SMEM] + [VMEM] * 2, sums, work, 3 << 20)(
        meta, held, got
    )
    grads = grads + swap(grads, 2)
    own, grads = lax.optimization_barrier((own, grads))
    low, high = (
        call(functools.partial(half_kernel, first), [(half, BF16)], [VMEM] * 3)(own, near, far)[0]
        for first, far in ((0, far_low), (HALF, far_high))
    )
    high, grads = lax.optimization_barrier((high, grads))
    low = move(low, lambda b, r: (b - 4 * r, r))
    high = move(high, lambda b, r: (b - 4 * r, r ^ 2))
    planes = exchange(jnp.broadcast_to(grads[None], (Z, GRAD, T)), "z")
    send, grads = call(
        gather_kernel, [((ROWS, T + 32, T), BF16), ((GRAD, T), F32)], [VMEM] * 3
    )(low, high, planes)
    got = exchange(send, REP)
    grad_features, grad_weight, grad_bias = call(
        last_kernel,
        [((T, T), F32), ((T, 2 * T), F32), ((1, 2 * T), F32)],
        [VMEM] * 3,
    )(got, scale, grads)
    return act, grad_weight, grad_bias[0], grad_features


def solution(mesh):
    fine = Mesh(mesh.devices.reshape(Z, YL, CORE, X, YH), BLK + REP)
    return jax.shard_map(
        on_device,
        mesh=fine,
        in_specs=(
            P(BLK, None),
            P(BLK),
            P(BLK, REP, None),
            P(BLK, REP),
            P(BLK, REP, None, None, None),
            P(),
            P(),
            P(BLK + REP, None),
        ),
        out_specs=(P(BLK + REP, None), P(), P(), P(BLK + REP, None)),
        check_vma=False,
    )
```

```python
import functools

import jax
import jax.numpy as jnp
from jax import lax
from jax.experimental import pallas as pl
from jax.experimental.pallas import tpu as pltpu
from jax.sharding import Mesh
from jax.sharding import PartitionSpec as P

Z, YL, CORE, X, YH = 8, 2, 2, 4, 2
BLK = ("z", "yl", "core")
REP = ("x", "yh")
T = 128
ROWS = 8
STEPS = 4
SLOTS = 6
HALF = ROWS // 2
NODES = ROWS * T
GRAD = 48
SWAP = 96
F32 = jnp.float32
BF16 = jnp.bfloat16

VMEM = pl.BlockSpec(memory_space=pltpu.VMEM)
SMEM = pl.BlockSpec(memory_space=pltpu.SMEM)
HBM = pl.BlockSpec(memory_space=pltpu.HBM)
PARAMS = pltpu.CompilerParams(vmem_limit_bytes=32 * 1024 * 1024)


def bias_rows(total):
    high = total.astype(BF16)
    low = (total - high.astype(F32)).astype(BF16)
    return jnp.concatenate([high, low, jnp.zeros((12, T), BF16)], axis=0)


def prologue_kernel(rep, features, degrees, low, high, scale):
    rows = jnp.concatenate([degrees[...].astype(F32), jnp.ones((T - ROWS, T), F32)], axis=0)
    columns = lax.rsqrt(rows.T)
    for j in range(ROWS):
        inv_root = jnp.broadcast_to(columns[:, j : j + 1], (T, T))
        tile = (features[j * T : (j + 1) * T].astype(F32) * inv_root).astype(BF16)
        half = low if j < HALF else high
        half[j % HALF] = tile

        @pl.when(rep[0] == j)
        def _():
            scale[...] = inv_root


def tile_of(low, high):
    def tile_at(col):
        at = lax.rem(col, HALF)
        return jnp.where(col < HALF, low[at], high[at])

    return tile_at


def product(meta, edges, i, s, tile_at):
    picked = []
    for c in range(SLOTS):
        tile = tile_at(meta[c, s, i])
        picked.append(jnp.where(c < meta[6, s, i], tile, jnp.zeros_like(tile)))
    left = jnp.concatenate([edges[i, s, c] for c in range(SLOTS)], axis=1)
    return jnp.dot(left, jnp.concatenate(picked, axis=0), preferred_element_type=F32)


def load_kernel(edges, held, sem):
    copy = pltpu.make_async_copy(edges, held, sem)
    copy.start()
    copy.wait()


def first_kernel(meta, held, low, high, out):
    for i in range(ROWS):
        out[i] = product(meta, held, i, 0, tile_of(low, high))


def second_kernel(meta, held, low, high, total, out):
    for i in range(ROWS):
        out[i] = total[i] + product(meta, held, i, 2, tile_of(low, high))


def third_kernel(meta, held, near_low, near_high, last_low, last_high, total, out):
    odd = meta[7, 0, 0]
    for i in range(ROWS):
        out[i] = (
            total[i]
            + product(meta, held, i, 3 - 2 * odd, tile_of(near_low, near_high))
            + product(meta, held, i, 1 + 2 * odd, tile_of(last_low, last_high))
        ).astype(BF16)


def dense_kernel(parts, scale, weight, bias, cot, act, send):
    total = parts[0].astype(F32)
    for j in range(1, ROWS):
        total += parts[j].astype(F32)
    agg = (scale[...] * total).astype(BF16)
    pre = jnp.dot(agg, weight[...], preferred_element_type=F32) + bias[...]
    sigma = jax.nn.sigmoid(pre)
    act[...] = (pre * sigma).astype(BF16)
    grad_pre = cot[...].astype(F32) * sigma * (1.0 + pre * (1.0 - sigma))
    half = grad_pre.astype(BF16)
    grad_w = lax.dot_general(agg, half, (((0,), (0,)), ((), ())), preferred_element_type=F32)
    grad_b = jnp.sum(grad_pre, axis=0, keepdims=True)
    grad_b = jnp.concatenate([grad_b[:, :T], grad_b[:, T:]], axis=0)
    back = lax.dot_general(
        half, weight[...], (((1,), (1,)), ((), ())), preferred_element_type=F32
    )
    back = (scale[...] * back).astype(BF16)
    rows_b = bias_rows(grad_b)
    grad_w = grad_w.astype(BF16)
    for j in range(ROWS):
        send[j, 0:T] = back
        send[j, T : T + 16] = grad_w[16 * j : 16 * j + 16, :T]
        send[j, T + 16 : T + 32] = grad_w[16 * j : 16 * j + 16, T:]
        send[j, T + 32 : T + 48] = rows_b


def column_sums(meta, held, got, s, sums):
    sums[...] = jnp.zeros_like(sums)
    for i in range(ROWS):
        back = got[i, 0:T].T
        right = jnp.concatenate([held[i, s, c] for c in range(SLOTS)], axis=1)
        prod = jnp.dot(back, right, preferred_element_type=F32)
        for c in range(SLOTS):
            part = prod[:, c * T : (c + 1) * T]
            at = meta[c, s, i]
            sums[at] += jnp.where(c < meta[6, s, i], part, jnp.zeros_like(part))


def near_sums_kernel(meta, held, got, near, last, sums):
    total = got[0, T:].astype(F32)
    for j in range(1, ROWS):
        total += got[j, T:].astype(F32)
    total = jnp.concatenate(
        [total[0:32], total[32:34] + total[34:36], jnp.zeros((14, T), F32)], axis=0
    )
    high = total.astype(BF16)
    last[NODES : NODES + GRAD] = high
    last[NODES + GRAD :] = (total - high.astype(F32)).astype(BF16)
    column_sums(meta, held, got, 1 + 2 * meta[7, 0, 0], sums)
    last[0:NODES] = sums[...].astype(BF16).reshape(NODES, T)
    column_sums(meta, held, got, 3 - 2 * meta[7, 0, 0], sums)
    near[...] = sums[...].astype(BF16)


def far_sums_kernel(meta, held, got, far, sums):
    column_sums(meta, held, got, 2, sums)
    far[...] = sums[...].astype(BF16)


def own_sums_kernel(meta, held, got, out, sums):
    column_sums(meta, held, got, 0, sums)
    out[...] = sums[...]


def grads_of(rows):
    return rows[NODES : NODES + GRAD].astype(F32) + rows[NODES + GRAD :].astype(F32)


def near_kernel(far, mine, other, low, high, grads):
    for j in range(ROWS):
        half = low if j < HALF else high
        rows = other[j * T : (j + 1) * T].astype(F32)
        half[j % HALF] = (far[j].astype(F32) + rows).astype(BF16)
    grads[0:GRAD] = grads_of(mine) + grads_of(other)
    grads[GRAD:] = jnp.zeros((SWAP - GRAD, T), F32)


def half_kernel(first, own, near, far, out):
    rows = pl.ds(first, HALF)
    total = own[rows] + near[rows].astype(F32) + far[...].astype(F32)
    out[...] = total.astype(BF16)


def gather_kernel(low, high, grads, out):
    mine = grads[0:32].astype(BF16)
    for j in range(ROWS):
        out[j, 0:T] = low[j] if j < HALF else high[j - HALF]
        out[j, T:] = mine


def last_kernel(got, scale, grads, grad_features, grad_weight, grad_bias):
    total = got[0, 0:T].astype(F32)
    for j in range(1, ROWS):
        total += got[j, 0:T].astype(F32)
    grad_features[...] = scale[...] * total.T
    for j in range(ROWS):
        rows = slice(16 * j, 16 * j + 16)
        grad_weight[rows, :T] = got[j, T : T + 16].astype(F32)
        grad_weight[rows, T:] = got[j, T + 16 :].astype(F32)
    grad_bias[...] = jnp.concatenate([grads[32:33], grads[33:34]], axis=1)


def call(kernel, out, in_specs, scratch=(), flops=0, moved=1 << 20):
    return pl.pallas_call(
        kernel,
        out_shape=[jax.ShapeDtypeStruct(*o) for o in out],
        in_specs=in_specs,
        out_specs=[VMEM] * len(out),
        scratch_shapes=list(scratch),
        cost_estimate=pl.CostEstimate(flops=flops, bytes_accessed=moved, transcendentals=0),
        compiler_params=PARAMS,
    )


def pinned(value):
    return pltpu.with_memory_space_constraint(value, pltpu.HBM)


def exchange(value, axes):
    return lax.all_to_all(value, axes, 0, 0, tiled=True)


def move(value, to):
    blk, rep = Z * YL * CORE, X * YH
    pairs = []
    for b in range(blk):
        for r in range(rep):
            to_b, to_r = to(b, r)
            pairs.append((b * rep + r, to_b % blk * rep + to_r))
    return lax.ppermute(value, BLK + REP, pairs)


def swap(value, bit):
    return move(value, lambda b, r: (b ^ bit, r))


def on_device(features, degrees, cols, counts, edges, weight, bias, cot):
    z, yl, core = (lax.axis_index(a) for a in BLK)
    rep = lax.axis_index(REP)
    place = lax.broadcasted_iota(jnp.int32, (1, STEPS, ROWS), 2)
    place = jnp.where(place == 0, core, 0)
    meta = jnp.concatenate([cols.transpose(2, 1, 0), counts.T[None], place], axis=0)

    tiles, half = (ROWS, T, T), (HALF, T, T)
    low, high, scale = call(
        prologue_kernel,
        [(half, BF16), (half, BF16), ((T, T), F32)],
        [SMEM, VMEM, VMEM],
    )(rep.astype(jnp.int32)[None], pinned(features), pinned(degrees.reshape(ROWS, T)))

    low = move(low, lambda b, r: (b + 4 * r, r))
    high = move(high, lambda b, r: (b + 4 * (r ^ 2), r ^ 2))
    (held,) = call(
        load_kernel, [(edges.shape, BF16)], [HBM], [pltpu.SemaphoreType.DMA], 0, 12 << 20
    )(pinned(edges))
    low, held, meta = lax.optimization_barrier((low, held, meta))
    far_low, far_high = (move(v, lambda b, r: (b + 2, r)) for v in (low, high))
    near_low = move(low, lambda b, r: (b + 1 + 2 * (b % 2), r))

    work = 2 * ROWS * SLOTS * T * T * T
    (total,) = call(first_kernel, [(tiles, F32)], [SMEM] + [VMEM] * 3, (), work, 3 << 20)(
        meta, held, low, high
    )
    high, total = lax.optimization_barrier((high, total))
    near_high = move(high, lambda b, r: (b + 1 + 2 * (b % 2), r))
    last_low, last_high = swap(far_low, 1), swap(far_high, 1)
    (total,) = call(second_kernel, [(tiles, F32)], [SMEM] + [VMEM] * 4, (), work, 3 << 20)(
        meta, held, far_low, far_high, total
    )
    (parts,) = call(third_kernel, [(tiles, BF16)], [SMEM] + [VMEM] * 6, (), 2 * work, 6 << 20)(
        meta, held, near_low, near_high, last_low, last_high, total
    )
    parts = exchange(parts, REP)

    act, send = call(
        dense_kernel,
        [(cot.shape, BF16), ((ROWS, T + GRAD, T), BF16)],
        [VMEM] * 5,
    )(parts, scale, weight, bias[None], cot)
    got = exchange(send, REP)

    sums = [pltpu.VMEM(tiles, F32)]
    near, mine = call(
        near_sums_kernel,
        [(tiles, BF16), ((NODES + 2 * GRAD, T), BF16)],
        [SMEM, VMEM, VMEM],
        sums,
        2 * work,
        6 << 20,
    )(meta, held, got)
    other = swap(mine, 1)
    near = move(near, lambda b, r: (b - 3 + 2 * (b % 2), r))
    (far,) = call(far_sums_kernel, [(tiles, BF16)], [SMEM, VMEM, VMEM], sums, work, 3 << 20)(
        meta, held, got
    )
    far_low, far_high, grads = call(
        near_kernel, [(half, BF16), (half, BF16), ((SWAP, T), F32)], [VMEM] * 3
    )(far, mine, other)
    far_low, far_high, got, grads = lax.optimization_barrier((far_low, far_high, got, grads))
    far_low, far_high = (move(v, lambda b, r: (b - 2, r)) for v in (far_low, far_high))
    (own,) = call(own_sums_kernel, [(tiles, F32)], [SMEM] + [VMEM] * 2, sums, work, 3 << 20)(
        meta, held, got
    )
    grads = grads + swap(grads, 2)
    own, grads = lax.optimization_barrier((own, grads))
    low, high = (
        call(functools.partial(half_kernel, first), [(half, BF16)], [VMEM] * 3)(own, near, far)[0]
        for first, far in ((0, far_low), (HALF, far_high))
    )
    low = move(low, lambda b, r: (b - 4 * r, r))
    high = move(high, lambda b, r: (b - 4 * r, r ^ 2))
    for bit in (16, 4, 8):
        grads = grads + swap(grads, bit)
    (send,) = call(gather_kernel, [((ROWS, T + 32, T), BF16)], [VMEM] * 3)(low, high, grads)
    got = exchange(send, REP)
    grad_features, grad_weight, grad_bias = call(
        last_kernel,
        [((T, T), F32), ((T, 2 * T), F32), ((1, 2 * T), F32)],
        [VMEM] * 3,
    )(got, scale, grads)
    return act, grad_weight, grad_bias[0], grad_features


def solution(mesh):
    fine = Mesh(mesh.devices.reshape(Z, YL, CORE, X, YH), BLK + REP)
    return jax.shard_map(
        on_device,
        mesh=fine,
        in_specs=(
            P(BLK, None),
            P(BLK),
            P(BLK, REP, None),
            P(BLK, REP),
            P(BLK, REP, None, None, None),
            P(),
            P(),
            P(BLK + REP, None),
        ),
        out_specs=(P(BLK + REP, None), P(), P(), P(BLK + REP, None)),
        check_vma=False,
    )
```

```python
import functools

import jax
import jax.numpy as jnp
from jax import lax
from jax.experimental import pallas as pl
from jax.experimental.pallas import tpu as pltpu
from jax.sharding import Mesh
from jax.sharding import PartitionSpec as P

Z, YL, CORE, X, YH = 8, 2, 2, 4, 2
BLK = ("z", "yl", "core")
REP = ("x", "yh")
T = 128
ROWS = 8
STEPS = 4
SLOTS = 6
HALF = ROWS // 2
NODES = ROWS * T
PAIR_FLOPS, GROUP_FLOPS = 5 * 10**9, 2 * 10**10
GRAD = 48
F32 = jnp.float32
BF16 = jnp.bfloat16

VMEM = pl.BlockSpec(memory_space=pltpu.VMEM)
SMEM = pl.BlockSpec(memory_space=pltpu.SMEM)
HBM = pl.BlockSpec(memory_space=pltpu.HBM)
PARAMS = pltpu.CompilerParams(vmem_limit_bytes=32 * 1024 * 1024)


def bias_rows(total):
    high = total.astype(BF16)
    low = (total - high.astype(F32)).astype(BF16)
    return jnp.concatenate([high, low, jnp.zeros((12, T), BF16)], axis=0)


def prologue_kernel(rep, features, degrees, low, high, scale):
    rows = jnp.concatenate([degrees[...].astype(F32), jnp.ones((T - ROWS, T), F32)], axis=0)
    columns = lax.rsqrt(rows.T)
    for j in range(ROWS):
        inv_root = jnp.broadcast_to(columns[:, j : j + 1], (T, T))
        tile = (features[j * T : (j + 1) * T].astype(F32) * inv_root).astype(BF16)
        half = low if j < HALF else high
        half[j % HALF] = tile

        @pl.when(rep[0] == j)
        def _():
            scale[...] = inv_root


def tile_of(low, high):
    def tile_at(col):
        at = lax.rem(col, HALF)
        return jnp.where(col < HALF, low[at], high[at])

    return tile_at


def product(meta, edges, i, s, tile_at):
    picked = []
    for c in range(SLOTS):
        tile = tile_at(meta[c, s, i])
        picked.append(jnp.where(c < meta[6, s, i], tile, jnp.zeros_like(tile)))
    left = jnp.concatenate([edges[i, s, c] for c in range(SLOTS)], axis=1)
    return jnp.dot(left, jnp.concatenate(picked, axis=0), preferred_element_type=F32)


def load_kernel(edges, held, sem):
    copy = pltpu.make_async_copy(edges, held, sem)
    copy.start()
    copy.wait()


def first_kernel(meta, held, low, high, out):
    for i in range(ROWS):
        out[i] = product(meta, held, i, 0, tile_of(low, high))


def second_kernel(meta, held, low, high, total, out):
    for i in range(ROWS):
        out[i] = total[i] + product(meta, held, i, 2, tile_of(low, high))


def third_kernel(meta, held, near_low, near_high, last_low, last_high, total, out):
    odd = meta[7, 0, 0]
    for i in range(ROWS):
        out[i] = (
            total[i]
            + product(meta, held, i, 3 - 2 * odd, tile_of(near_low, near_high))
            + product(meta, held, i, 1 + 2 * odd, tile_of(last_low, last_high))
        ).astype(BF16)


def dense_kernel(parts, scale, weight, bias, cot, act, send):
    total = parts[0].astype(F32)
    for j in range(1, ROWS):
        total += parts[j].astype(F32)
    agg = (scale[...] * total).astype(BF16)
    pre = jnp.dot(agg, weight[...], preferred_element_type=F32) + bias[...]
    sigma = jax.nn.sigmoid(pre)
    act[...] = (pre * sigma).astype(BF16)
    grad_pre = cot[...].astype(F32) * sigma * (1.0 + pre * (1.0 - sigma))
    half = grad_pre.astype(BF16)
    grad_w = lax.dot_general(agg, half, (((0,), (0,)), ((), ())), preferred_element_type=F32)
    grad_b = jnp.sum(grad_pre, axis=0, keepdims=True)
    grad_b = jnp.concatenate([grad_b[:, :T], grad_b[:, T:]], axis=0)
    back = lax.dot_general(
        half, weight[...], (((1,), (1,)), ((), ())), preferred_element_type=F32
    )
    back = (scale[...] * back).astype(BF16)
    rows_b = bias_rows(grad_b)
    grad_w = grad_w.astype(BF16)
    for j in range(ROWS):
        send[j, 0:T] = back
        send[j, T : T + 16] = grad_w[16 * j : 16 * j + 16, :T]
        send[j, T + 16 : T + 32] = grad_w[16 * j : 16 * j + 16, T:]
        send[j, T + 32 : T + 48] = rows_b


def column_sums(meta, held, got, s, sums):
    sums[...] = jnp.zeros_like(sums)
    for i in range(ROWS):
        back = got[i, 0:T].T
        right = jnp.concatenate([held[i, s, c] for c in range(SLOTS)], axis=1)
        prod = jnp.dot(back, right, preferred_element_type=F32)
        for c in range(SLOTS):
            part = prod[:, c * T : (c + 1) * T]
            at = meta[c, s, i]
            sums[at] += jnp.where(c < meta[6, s, i], part, jnp.zeros_like(part))


def near_sums_kernel(meta, held, got, near, last, sums):
    total = got[0, T:].astype(F32)
    for j in range(1, ROWS):
        total += got[j, T:].astype(F32)
    total = jnp.concatenate(
        [total[0:32], total[32:34] + total[34:36], jnp.zeros((14, T), F32)], axis=0
    )
    high = total.astype(BF16)
    last[NODES : NODES + GRAD] = high
    last[NODES + GRAD :] = (total - high.astype(F32)).astype(BF16)
    column_sums(meta, held, got, 1 + 2 * meta[7, 0, 0], sums)
    last[0:NODES] = sums[...].astype(BF16).reshape(NODES, T)
    column_sums(meta, held, got, 3 - 2 * meta[7, 0, 0], sums)
    near[...] = sums[...].astype(BF16)


def far_sums_kernel(meta, held, got, far, sums):
    column_sums(meta, held, got, 2, sums)
    far[...] = sums[...].astype(BF16)


def own_sums_kernel(meta, held, got, out, sums):
    column_sums(meta, held, got, 0, sums)
    out[...] = sums[...]


def grads_of(rows):
    return rows[NODES : NODES + GRAD].astype(F32) + rows[NODES + GRAD :].astype(F32)


def near_kernel(far, other, low, high):
    for j in range(ROWS):
        half = low if j < HALF else high
        rows = other[j * T : (j + 1) * T].astype(F32)
        half[j % HALF] = (far[j].astype(F32) + rows).astype(BF16)


def pair_kernel(mine, other, grads):
    grads[...] = grads_of(mine) + grads_of(other)


def group_kernel(grads, one, two, three, low, high, out):
    out[...] = (grads[...] + one[...]) + (two[...] + three[...])


def half_kernel(first, own, near, far, out):
    rows = pl.ds(first, HALF)
    total = own[rows] + near[rows].astype(F32) + far[...].astype(F32)
    out[...] = total.astype(BF16)


def gather_kernel(low, high, grads, out):
    mine = grads[0:32].astype(BF16)
    for j in range(ROWS):
        out[j, 0:T] = low[j] if j < HALF else high[j - HALF]
        out[j, T:] = mine


def last_kernel(got, scale, grads, grad_features, grad_weight, grad_bias):
    total = got[0, 0:T].astype(F32)
    for j in range(1, ROWS):
        total += got[j, 0:T].astype(F32)
    grad_features[...] = scale[...] * total.T
    for j in range(ROWS):
        rows = slice(16 * j, 16 * j + 16)
        grad_weight[rows, :T] = got[j, T : T + 16].astype(F32)
        grad_weight[rows, T:] = got[j, T + 16 :].astype(F32)
    grad_bias[...] = jnp.concatenate([grads[32:33], grads[33:34]], axis=1)


def call(kernel, out, in_specs, scratch=(), flops=0, moved=1 << 20):
    return pl.pallas_call(
        kernel,
        out_shape=[jax.ShapeDtypeStruct(*o) for o in out],
        in_specs=in_specs,
        out_specs=[VMEM] * len(out),
        scratch_shapes=list(scratch),
        cost_estimate=pl.CostEstimate(flops=flops, bytes_accessed=moved, transcendentals=0),
        compiler_params=PARAMS,
    )


def pinned(value):
    return pltpu.with_memory_space_constraint(value, pltpu.HBM)


def exchange(value, axes):
    return lax.all_to_all(value, axes, 0, 0, tiled=True)


def move(value, to):
    blk, rep = Z * YL * CORE, X * YH
    pairs = []
    for b in range(blk):
        for r in range(rep):
            to_b, to_r = to(b, r)
            pairs.append((b * rep + r, to_b % blk * rep + to_r))
    return lax.ppermute(value, BLK + REP, pairs)


def swap(value, bit):
    return move(value, lambda b, r: (b ^ bit, r))


def on_device(features, degrees, cols, counts, edges, weight, bias, cot):
    z, yl, core = (lax.axis_index(a) for a in BLK)
    rep = lax.axis_index(REP)
    place = lax.broadcasted_iota(jnp.int32, (1, STEPS, ROWS), 2)
    place = jnp.where(place == 0, core, 0)
    meta = jnp.concatenate([cols.transpose(2, 1, 0), counts.T[None], place], axis=0)

    tiles, half = (ROWS, T, T), (HALF, T, T)
    low, high, scale = call(
        prologue_kernel,
        [(half, BF16), (half, BF16), ((T, T), F32)],
        [SMEM, VMEM, VMEM],
    )(rep.astype(jnp.int32)[None], pinned(features), pinned(degrees.reshape(ROWS, T)))

    low = move(low, lambda b, r: (b + 4 * r, r))
    high = move(high, lambda b, r: (b + 4 * (r ^ 2), r ^ 2))
    (held,) = call(
        load_kernel, [(edges.shape, BF16)], [HBM], [pltpu.SemaphoreType.DMA], 0, 12 << 20
    )(pinned(edges))
    low, held, meta = lax.optimization_barrier((low, held, meta))
    far_low, far_high = (move(v, lambda b, r: (b + 2, r)) for v in (low, high))
    near_low = move(low, lambda b, r: (b + 1 + 2 * (b % 2), r))

    work = 2 * ROWS * SLOTS * T * T * T
    (total,) = call(first_kernel, [(tiles, F32)], [SMEM] + [VMEM] * 3, (), work, 3 << 20)(
        meta, held, low, high
    )
    high, total = lax.optimization_barrier((high, total))
    near_high = move(high, lambda b, r: (b + 1 + 2 * (b % 2), r))
    last_low, last_high = swap(far_low, 1), swap(far_high, 1)
    (total,) = call(second_kernel, [(tiles, F32)], [SMEM] + [VMEM] * 4, (), work, 3 << 20)(
        meta, held, far_low, far_high, total
    )
    (parts,) = call(third_kernel, [(tiles, BF16)], [SMEM] + [VMEM] * 6, (), 2 * work, 6 << 20)(
        meta, held, near_low, near_high, last_low, last_high, total
    )
    parts = exchange(parts, REP)

    act, send = call(
        dense_kernel,
        [(cot.shape, BF16), ((ROWS, T + GRAD, T), BF16)],
        [VMEM] * 5,
    )(parts, scale, weight, bias[None], cot)
    got = exchange(send, REP)

    sums = [pltpu.VMEM(tiles, F32)]
    near, mine = call(
        near_sums_kernel,
        [(tiles, BF16), ((NODES + 2 * GRAD, T), BF16)],
        [SMEM, VMEM, VMEM],
        sums,
        2 * work,
        6 << 20,
    )(meta, held, got)
    other = swap(mine, 1)
    near = move(near, lambda b, r: (b - 3 + 2 * (b % 2), r))
    (far,) = call(far_sums_kernel, [(tiles, BF16)], [SMEM, VMEM, VMEM], sums, work, 3 << 20)(
        meta, held, got
    )
    far_low, far_high = call(near_kernel, [(half, BF16), (half, BF16)], [VMEM] * 2)(far, other)
    far_low, far_high, got, other = lax.optimization_barrier((far_low, far_high, got, other))
    far_low, far_high = (move(v, lambda b, r: (b - 2, r)) for v in (far_low, far_high))
    (own,) = call(own_sums_kernel, [(tiles, F32)], [SMEM] + [VMEM] * 2, sums, work, 3 << 20)(
        meta, held, got
    )
    (grads,) = call(pair_kernel, [((GRAD, T), F32)], [VMEM] * 2, (), PAIR_FLOPS)(mine, other)
    groups = [swap(grads, bits) for bits in (4, 8, 12)]
    low, high = (
        call(functools.partial(half_kernel, first), [(half, BF16)], [VMEM] * 3)(own, near, far)[0]
        for first, far in ((0, far_low), (HALF, far_high))
    )
    sent_low, sent_high = low, high
    low = move(low, lambda b, r: (b - 4 * r, r))
    high = move(high, lambda b, r: (b - 4 * r, r ^ 2))
    anywhere = pl.BlockSpec(memory_space=pl.ANY)
    (grads,) = call(
        group_kernel, [((GRAD, T), F32)], [VMEM] * 4 + [anywhere] * 2, (), GROUP_FLOPS
    )(grads, *groups, sent_low, sent_high)
    for bit in (2, 16):
        grads = grads + swap(grads, bit)
    (send,) = call(gather_kernel, [((ROWS, T + 32, T), BF16)], [VMEM] * 3)(low, high, grads)
    got = exchange(send, REP)
    grad_features, grad_weight, grad_bias = call(
        last_kernel,
        [((T, T), F32), ((T, 2 * T), F32), ((1, 2 * T), F32)],
        [VMEM] * 3,
    )(got, scale, grads)
    return act, grad_weight, grad_bias[0], grad_features


def solution(mesh):
    fine = Mesh(mesh.devices.reshape(Z, YL, CORE, X, YH), BLK + REP)
    return jax.shard_map(
        on_device,
        mesh=fine,
        in_specs=(
            P(BLK, None),
            P(BLK),
            P(BLK, REP, None),
            P(BLK, REP),
            P(BLK, REP, None, None, None),
            P(),
            P(),
            P(BLK + REP, None),
        ),
        out_specs=(P(BLK + REP, None), P(), P(), P(BLK + REP, None)),
        check_vma=False,
    )
```

```python
import functools

import jax
import jax.numpy as jnp
from jax import lax
from jax.experimental import pallas as pl
from jax.experimental.pallas import tpu as pltpu
from jax.sharding import Mesh
from jax.sharding import PartitionSpec as P

Z, YL, CORE, X, YH = 8, 2, 2, 4, 2
BLK = ("z", "yl", "core")
REP = ("x", "yh")
T = 128
ROWS = 8
STEPS = 4
SLOTS = 6
HALF = ROWS // 2
NODES = ROWS * T
PAIR_FLOPS, GROUP_FLOPS = 5 * 10**9, 2 * 10**10
GRAD = 48
F32 = jnp.float32
BF16 = jnp.bfloat16

VMEM = pl.BlockSpec(memory_space=pltpu.VMEM)
SMEM = pl.BlockSpec(memory_space=pltpu.SMEM)
HBM = pl.BlockSpec(memory_space=pltpu.HBM)
PARAMS = pltpu.CompilerParams(vmem_limit_bytes=32 * 1024 * 1024)


def bias_rows(total):
    high = total.astype(BF16)
    low = (total - high.astype(F32)).astype(BF16)
    return jnp.concatenate([high, low, jnp.zeros((12, T), BF16)], axis=0)


def prologue_kernel(rep, features, degrees, low, high, scale):
    rows = jnp.concatenate([degrees[...].astype(F32), jnp.ones((T - ROWS, T), F32)], axis=0)
    columns = lax.rsqrt(rows.T)
    for j in range(ROWS):
        inv_root = jnp.broadcast_to(columns[:, j : j + 1], (T, T))
        tile = (features[j * T : (j + 1) * T].astype(F32) * inv_root).astype(BF16)
        half = low if j < HALF else high
        half[j % HALF] = tile

        @pl.when(rep[0] == j)
        def _():
            scale[...] = inv_root


def tile_of(low, high):
    def tile_at(col):
        at = lax.rem(col, HALF)
        return jnp.where(col < HALF, low[at], high[at])

    return tile_at


def product(meta, edges, i, s, tile_at):
    picked = []
    for c in range(SLOTS):
        tile = tile_at(meta[c, s, i])
        picked.append(jnp.where(c < meta[6, s, i], tile, jnp.zeros_like(tile)))
    left = jnp.concatenate([edges[i, s, c] for c in range(SLOTS)], axis=1)
    return jnp.dot(left, jnp.concatenate(picked, axis=0), preferred_element_type=F32)


def load_kernel(edges, held, sem):
    copy = pltpu.make_async_copy(edges, held, sem)
    copy.start()
    copy.wait()


def first_kernel(meta, held, low, high, out):
    for i in range(ROWS):
        out[i] = product(meta, held, i, 0, tile_of(low, high))


def second_kernel(meta, held, low, high, total, out):
    for i in range(ROWS):
        out[i] = total[i] + product(meta, held, i, 2, tile_of(low, high))


def third_kernel(meta, held, near_low, near_high, last_low, last_high, total, out):
    odd = meta[7, 0, 0]
    for i in range(ROWS):
        out[i] = (
            total[i]
            + product(meta, held, i, 3 - 2 * odd, tile_of(near_low, near_high))
            + product(meta, held, i, 1 + 2 * odd, tile_of(last_low, last_high))
        ).astype(BF16)


def dense_kernel(parts, scale, weight, bias, cot, act, send):
    total = parts[0].astype(F32)
    for j in range(1, ROWS):
        total += parts[j].astype(F32)
    agg = (scale[...] * total).astype(BF16)
    pre = jnp.dot(agg, weight[...], preferred_element_type=F32) + bias[...]
    sigma = jax.nn.sigmoid(pre)
    act[...] = (pre * sigma).astype(BF16)
    grad_pre = cot[...].astype(F32) * sigma * (1.0 + pre * (1.0 - sigma))
    half = grad_pre.astype(BF16)
    grad_w = lax.dot_general(agg, half, (((0,), (0,)), ((), ())), preferred_element_type=F32)
    grad_b = jnp.sum(grad_pre, axis=0, keepdims=True)
    grad_b = jnp.concatenate([grad_b[:, :T], grad_b[:, T:]], axis=0)
    back = lax.dot_general(
        half, weight[...], (((1,), (1,)), ((), ())), preferred_element_type=F32
    )
    back = (scale[...] * back).astype(BF16)
    rows_b = bias_rows(grad_b)
    grad_w = grad_w.astype(BF16)
    for j in range(ROWS):
        send[j, 0:T] = back
        send[j, T : T + 16] = grad_w[16 * j : 16 * j + 16, :T]
        send[j, T + 16 : T + 32] = grad_w[16 * j : 16 * j + 16, T:]
        send[j, T + 32 : T + 48] = rows_b


def column_sums(meta, held, got, s, sums):
    sums[...] = jnp.zeros_like(sums)
    for i in range(ROWS):
        back = got[i, 0:T].T
        right = jnp.concatenate([held[i, s, c] for c in range(SLOTS)], axis=1)
        prod = jnp.dot(back, right, preferred_element_type=F32)
        for c in range(SLOTS):
            part = prod[:, c * T : (c + 1) * T]
            at = meta[c, s, i]
            sums[at] += jnp.where(c < meta[6, s, i], part, jnp.zeros_like(part))


def near_sums_kernel(meta, held, got, near, last, sums):
    total = got[0, T:].astype(F32)
    for j in range(1, ROWS):
        total += got[j, T:].astype(F32)
    total = jnp.concatenate(
        [total[0:32], total[32:34] + total[34:36], jnp.zeros((14, T), F32)], axis=0
    )
    high = total.astype(BF16)
    last[NODES : NODES + GRAD] = high
    last[NODES + GRAD :] = (total - high.astype(F32)).astype(BF16)
    column_sums(meta, held, got, 1 + 2 * meta[7, 0, 0], sums)
    last[0:NODES] = sums[...].astype(BF16).reshape(NODES, T)
    column_sums(meta, held, got, 3 - 2 * meta[7, 0, 0], sums)
    near[...] = sums[...].astype(BF16)


def far_sums_kernel(meta, held, got, far, sums):
    column_sums(meta, held, got, 2, sums)
    far[...] = sums[...].astype(BF16)


def own_sums_kernel(meta, held, got, out, sums):
    column_sums(meta, held, got, 0, sums)
    out[...] = sums[...]


def grads_of(rows):
    return rows[NODES : NODES + GRAD].astype(F32) + rows[NODES + GRAD :].astype(F32)


def near_kernel(far, other, out):
    for j in range(ROWS):
        rows = other[j * T : (j + 1) * T].astype(F32)
        out[j] = (far[j].astype(F32) + rows).astype(BF16)


def pair_kernel(mine, other, grads):
    grads[...] = grads_of(mine) + grads_of(other)


def group_kernel(grads, one, two, three, low, high, out):
    out[...] = (grads[...] + one[...]) + (two[...] + three[...])


def total_kernel(own, near, far, one, two, three, low, high):
    for half, first in ((low, 0), (high, HALF)):
        rows = pl.ds(first, HALF)
        total = own[rows] + near[rows].astype(F32) + far[rows].astype(F32)
        half[...] = total.astype(BF16)


def gather_kernel(low, high, grads, out):
    mine = grads[0:32].astype(BF16)
    for j in range(ROWS):
        out[j, 0:T] = low[j] if j < HALF else high[j - HALF]
        out[j, T:] = mine


def last_kernel(got, scale, grads, grad_features, grad_weight, grad_bias):
    total = got[0, 0:T].astype(F32)
    for j in range(1, ROWS):
        total += got[j, 0:T].astype(F32)
    grad_features[...] = scale[...] * total.T
    for j in range(ROWS):
        rows = slice(16 * j, 16 * j + 16)
        grad_weight[rows, :T] = got[j, T : T + 16].astype(F32)
        grad_weight[rows, T:] = got[j, T + 16 :].astype(F32)
    grad_bias[...] = jnp.concatenate([grads[32:33], grads[33:34]], axis=1)


def call(kernel, out, in_specs, scratch=(), flops=0, moved=1 << 20):
    return pl.pallas_call(
        kernel,
        out_shape=[jax.ShapeDtypeStruct(*o) for o in out],
        in_specs=in_specs,
        out_specs=[VMEM] * len(out),
        scratch_shapes=list(scratch),
        cost_estimate=pl.CostEstimate(flops=flops, bytes_accessed=moved, transcendentals=0),
        compiler_params=PARAMS,
    )


def pinned(value):
    return pltpu.with_memory_space_constraint(value, pltpu.HBM)


def exchange(value, axes):
    return lax.all_to_all(value, axes, 0, 0, tiled=True)


def move(value, to):
    blk, rep = Z * YL * CORE, X * YH
    pairs = []
    for b in range(blk):
        for r in range(rep):
            to_b, to_r = to(b, r)
            pairs.append((b * rep + r, to_b % blk * rep + to_r))
    return lax.ppermute(value, BLK + REP, pairs)


def column(r):
    return r ^ (6 if r % 2 else 2)


def swap(value, bit):
    return move(value, lambda b, r: (b ^ bit, r))


def on_device(features, degrees, cols, counts, edges, weight, bias, cot):
    z, yl, core = (lax.axis_index(a) for a in BLK)
    rep = lax.axis_index(REP)
    place = lax.broadcasted_iota(jnp.int32, (1, STEPS, ROWS), 2)
    place = jnp.where(place == 0, core, 0)
    meta = jnp.concatenate([cols.transpose(2, 1, 0), counts.T[None], place], axis=0)

    tiles, half = (ROWS, T, T), (HALF, T, T)
    low, high, scale = call(
        prologue_kernel,
        [(half, BF16), (half, BF16), ((T, T), F32)],
        [SMEM, VMEM, VMEM],
    )(rep.astype(jnp.int32)[None], pinned(features), pinned(degrees.reshape(ROWS, T)))

    low = move(low, lambda b, r: (b + 4 * r, r))
    high = move(high, lambda b, r: (b + 4 * column(r), column(r)))
    (held,) = call(
        load_kernel, [(edges.shape, BF16)], [HBM], [pltpu.SemaphoreType.DMA], 0, 12 << 20
    )(pinned(edges))
    low, held, meta = lax.optimization_barrier((low, held, meta))
    far_low, far_high = (move(v, lambda b, r: (b + 2, r)) for v in (low, high))
    near_low = move(low, lambda b, r: (b + 1 + 2 * (b % 2), r))

    work = 2 * ROWS * SLOTS * T * T * T
    (total,) = call(first_kernel, [(tiles, F32)], [SMEM] + [VMEM] * 3, (), work, 3 << 20)(
        meta, held, low, high
    )
    high, total = lax.optimization_barrier((high, total))
    near_high = move(high, lambda b, r: (b + 1 + 2 * (b % 2), r))
    last_low, last_high = swap(far_low, 1), swap(far_high, 1)
    (total,) = call(second_kernel, [(tiles, F32)], [SMEM] + [VMEM] * 4, (), work, 3 << 20)(
        meta, held, far_low, far_high, total
    )
    (parts,) = call(third_kernel, [(tiles, BF16)], [SMEM] + [VMEM] * 6, (), 2 * work, 6 << 20)(
        meta, held, near_low, near_high, last_low, last_high, total
    )
    parts = exchange(parts, REP)

    act, send = call(
        dense_kernel,
        [(cot.shape, BF16), ((ROWS, T + GRAD, T), BF16)],
        [VMEM] * 5,
    )(parts, scale, weight, bias[None], cot)
    got = exchange(send, REP)

    sums = [pltpu.VMEM(tiles, F32)]
    near, mine = call(
        near_sums_kernel,
        [(tiles, BF16), ((NODES + 2 * GRAD, T), BF16)],
        [SMEM, VMEM, VMEM],
        sums,
        2 * work,
        6 << 20,
    )(meta, held, got)
    other = swap(mine, 1)
    near = move(near, lambda b, r: (b - 3 + 2 * (b % 2), r))
    (far,) = call(far_sums_kernel, [(tiles, BF16)], [SMEM, VMEM, VMEM], sums, work, 3 << 20)(
        meta, held, got
    )
    (far,) = call(near_kernel, [(tiles, BF16)], [VMEM] * 2)(far, other)
    far, got, other = lax.optimization_barrier((far, got, other))
    far = move(far, lambda b, r: (b - 2, r))
    (own,) = call(own_sums_kernel, [(tiles, F32)], [SMEM] + [VMEM] * 2, sums, work, 3 << 20)(
        meta, held, got
    )
    (grads,) = call(pair_kernel, [((GRAD, T), F32)], [VMEM] * 2, (), PAIR_FLOPS)(mine, other)
    groups = [swap(grads, bits) for bits in (4, 8, 12)]
    anywhere = pl.BlockSpec(memory_space=pl.ANY)
    low, high = call(total_kernel, [(half, BF16), (half, BF16)], [VMEM] * 3 + [anywhere] * 3)(
        own, near, far, *groups
    )
    sent_low, sent_high = low, high
    low = move(low, lambda b, r: (b - 4 * r, r))
    high = move(high, lambda b, r: (b, column(r)))
    high = move(high, lambda b, r: (b - 4 * column(r), r))
    (grads,) = call(
        group_kernel, [((GRAD, T), F32)], [VMEM] * 4 + [anywhere] * 2, (), GROUP_FLOPS
    )(grads, *groups, sent_low, sent_high)
    for bit in (2, 16):
        grads = grads + swap(grads, bit)
    (send,) = call(gather_kernel, [((ROWS, T + 32, T), BF16)], [VMEM] * 3)(low, high, grads)
    got = exchange(send, REP)
    grad_features, grad_weight, grad_bias = call(
        last_kernel,
        [((T, T), F32), ((T, 2 * T), F32), ((1, 2 * T), F32)],
        [VMEM] * 3,
    )(got, scale, grads)
    return act, grad_weight, grad_bias[0], grad_features


def solution(mesh):
    fine = Mesh(mesh.devices.reshape(Z, YL, CORE, X, YH), BLK + REP)
    return jax.shard_map(
        on_device,
        mesh=fine,
        in_specs=(
            P(BLK, None),
            P(BLK),
            P(BLK, REP, None),
            P(BLK, REP),
            P(BLK, REP, None, None, None),
            P(),
            P(),
            P(BLK + REP, None),
        ),
        out_specs=(P(BLK + REP, None), P(), P(), P(BLK + REP, None)),
        check_vma=False,
    )
```

```python
import functools

import jax
import jax.numpy as jnp
from jax import lax
from jax.experimental import pallas as pl
from jax.experimental.pallas import tpu as pltpu
from jax.sharding import Mesh
from jax.sharding import PartitionSpec as P

Z, YL, CORE, X, YH = 8, 2, 2, 4, 2
BLK = ("z", "yl", "core")
REP = ("x", "yh")
T = 128
ROWS = 8
STEPS = 4
SLOTS = 6
HALF = ROWS // 2
NODES = ROWS * T
PAIR_FLOPS, GROUP_FLOPS = 5 * 10**9, 2 * 10**10
GRAD = 48
F32 = jnp.float32
BF16 = jnp.bfloat16

VMEM = pl.BlockSpec(memory_space=pltpu.VMEM)
SMEM = pl.BlockSpec(memory_space=pltpu.SMEM)
HBM = pl.BlockSpec(memory_space=pltpu.HBM)
PARAMS = pltpu.CompilerParams(vmem_limit_bytes=32 * 1024 * 1024)


def bias_rows(total):
    high = total.astype(BF16)
    low = (total - high.astype(F32)).astype(BF16)
    return jnp.concatenate([high, low, jnp.zeros((12, T), BF16)], axis=0)


def prologue_kernel(rep, features, degrees, low, high, scale):
    rows = jnp.concatenate([degrees[...].astype(F32), jnp.ones((T - ROWS, T), F32)], axis=0)
    columns = lax.rsqrt(rows.T)
    for j in range(ROWS):
        inv_root = jnp.broadcast_to(columns[:, j : j + 1], (T, T))
        tile = (features[j * T : (j + 1) * T].astype(F32) * inv_root).astype(BF16)
        half = low if j < HALF else high
        half[j % HALF] = tile

        @pl.when(rep[0] == j)
        def _():
            scale[...] = inv_root


def tile_of(low, high):
    def tile_at(col):
        at = lax.rem(col, HALF)
        return jnp.where(col < HALF, low[at], high[at])

    return tile_at


def product(meta, edges, i, s, tile_at):
    picked = []
    for c in range(SLOTS):
        tile = tile_at(meta[c, s, i])
        picked.append(jnp.where(c < meta[6, s, i], tile, jnp.zeros_like(tile)))
    left = jnp.concatenate([edges[i, s, c] for c in range(SLOTS)], axis=1)
    return jnp.dot(left, jnp.concatenate(picked, axis=0), preferred_element_type=F32)


def load_kernel(edges, held, sem):
    copy = pltpu.make_async_copy(edges, held, sem)
    copy.start()
    copy.wait()


def first_kernel(meta, held, low, high, out):
    for i in range(ROWS):
        out[i] = product(meta, held, i, 0, tile_of(low, high))


def second_kernel(meta, held, low, high, total, out):
    for i in range(ROWS):
        out[i] = total[i] + product(meta, held, i, 2, tile_of(low, high))


def third_kernel(meta, held, near_low, near_high, last_low, last_high, total, out):
    odd = meta[7, 0, 0]
    for i in range(ROWS):
        out[i] = (
            total[i]
            + product(meta, held, i, 3 - 2 * odd, tile_of(near_low, near_high))
            + product(meta, held, i, 1 + 2 * odd, tile_of(last_low, last_high))
        ).astype(BF16)


def dense_kernel(parts, scale, weight, bias, cot, act, send):
    total = parts[0].astype(F32)
    for j in range(1, ROWS):
        total += parts[j].astype(F32)
    agg = (scale[...] * total).astype(BF16)
    pre = jnp.dot(agg, weight[...], preferred_element_type=F32) + bias[...]
    sigma = jax.nn.sigmoid(pre)
    act[...] = (pre * sigma).astype(BF16)
    grad_pre = cot[...].astype(F32) * sigma * (1.0 + pre * (1.0 - sigma))
    half = grad_pre.astype(BF16)
    grad_w = lax.dot_general(agg, half, (((0,), (0,)), ((), ())), preferred_element_type=F32)
    grad_b = jnp.sum(grad_pre, axis=0, keepdims=True)
    grad_b = jnp.concatenate([grad_b[:, :T], grad_b[:, T:]], axis=0)
    back = lax.dot_general(
        half, weight[...], (((1,), (1,)), ((), ())), preferred_element_type=F32
    )
    back = (scale[...] * back).astype(BF16)
    rows_b = bias_rows(grad_b)
    grad_w = grad_w.astype(BF16)
    for j in range(ROWS):
        send[j, 0:T] = back
        send[j, T : T + 16] = grad_w[16 * j : 16 * j + 16, :T]
        send[j, T + 16 : T + 32] = grad_w[16 * j : 16 * j + 16, T:]
        send[j, T + 32 : T + 48] = rows_b


def column_sums(meta, held, got, s, sums):
    sums[...] = jnp.zeros_like(sums)
    for i in range(ROWS):
        back = got[i, 0:T].T
        right = jnp.concatenate([held[i, s, c] for c in range(SLOTS)], axis=1)
        prod = jnp.dot(back, right, preferred_element_type=F32)
        for c in range(SLOTS):
            part = prod[:, c * T : (c + 1) * T]
            at = meta[c, s, i]
            sums[at] += jnp.where(c < meta[6, s, i], part, jnp.zeros_like(part))


def near_sums_kernel(meta, held, got, near, last, sums):
    total = got[0, T:].astype(F32)
    for j in range(1, ROWS):
        total += got[j, T:].astype(F32)
    total = jnp.concatenate(
        [total[0:32], total[32:34] + total[34:36], jnp.zeros((14, T), F32)], axis=0
    )
    high = total.astype(BF16)
    last[NODES : NODES + GRAD] = high
    last[NODES + GRAD :] = (total - high.astype(F32)).astype(BF16)
    column_sums(meta, held, got, 1 + 2 * meta[7, 0, 0], sums)
    last[0:NODES] = sums[...].astype(BF16).reshape(NODES, T)
    column_sums(meta, held, got, 3 - 2 * meta[7, 0, 0], sums)
    near[...] = sums[...].astype(BF16)


def far_sums_kernel(meta, held, got, far, sums):
    column_sums(meta, held, got, 2, sums)
    far[...] = sums[...].astype(BF16)


def own_sums_kernel(meta, held, got, out, sums):
    column_sums(meta, held, got, 0, sums)
    out[...] = sums[...]


def grads_of(rows):
    return rows[NODES : NODES + GRAD].astype(F32) + rows[NODES + GRAD :].astype(F32)


def near_kernel(far, other, out):
    for j in range(ROWS):
        rows = other[j * T : (j + 1) * T].astype(F32)
        out[j] = (far[j].astype(F32) + rows).astype(BF16)


def pair_kernel(mine, other, grads):
    grads[...] = grads_of(mine) + grads_of(other)


def group_kernel(grads, one, two, three, low, high, out):
    out[...] = (grads[...] + one[...]) + (two[...] + three[...])


def total_kernel(own, near, far, low, high):
    for half, first in ((low, 0), (high, HALF)):
        rows = pl.ds(first, HALF)
        total = own[rows] + near[rows].astype(F32) + far[rows].astype(F32)
        half[...] = total.astype(BF16)


def gather_kernel(low, high, grads, out):
    mine = grads[0:32].astype(BF16)
    for j in range(ROWS):
        out[j, 0:T] = low[j] if j < HALF else high[j - HALF]
        out[j, T:] = mine


def last_kernel(got, scale, grads, grad_features, grad_weight, grad_bias):
    total = got[0, 0:T].astype(F32)
    for j in range(1, ROWS):
        total += got[j, 0:T].astype(F32)
    grad_features[...] = scale[...] * total.T
    for j in range(ROWS):
        rows = slice(16 * j, 16 * j + 16)
        grad_weight[rows, :T] = got[j, T : T + 16].astype(F32)
        grad_weight[rows, T:] = got[j, T + 16 :].astype(F32)
    grad_bias[...] = jnp.concatenate([grads[32:33], grads[33:34]], axis=1)


def call(kernel, out, in_specs, scratch=(), flops=0, moved=1 << 20):
    return pl.pallas_call(
        kernel,
        out_shape=[jax.ShapeDtypeStruct(*o) for o in out],
        in_specs=in_specs,
        out_specs=[VMEM] * len(out),
        scratch_shapes=list(scratch),
        cost_estimate=pl.CostEstimate(flops=flops, bytes_accessed=moved, transcendentals=0),
        compiler_params=PARAMS,
    )


def pinned(value):
    return pltpu.with_memory_space_constraint(value, pltpu.HBM)


def exchange(value, axes):
    return lax.all_to_all(value, axes, 0, 0, tiled=True)


def move(value, to):
    blk, rep = Z * YL * CORE, X * YH
    pairs = []
    for b in range(blk):
        for r in range(rep):
            to_b, to_r = to(b, r)
            pairs.append((b * rep + r, to_b % blk * rep + to_r))
    return lax.ppermute(value, BLK + REP, pairs)


def column(r):
    return r ^ (6 if r % 2 else 2)


def swap(value, bit):
    return move(value, lambda b, r: (b ^ bit, r))


def on_device(features, degrees, cols, counts, edges, weight, bias, cot):
    z, yl, core = (lax.axis_index(a) for a in BLK)
    rep = lax.axis_index(REP)
    place = lax.broadcasted_iota(jnp.int32, (1, STEPS, ROWS), 2)
    place = jnp.where(place == 0, core, 0)
    meta = jnp.concatenate([cols.transpose(2, 1, 0), counts.T[None], place], axis=0)

    tiles, half = (ROWS, T, T), (HALF, T, T)
    low, high, scale = call(
        prologue_kernel,
        [(half, BF16), (half, BF16), ((T, T), F32)],
        [SMEM, VMEM, VMEM],
    )(rep.astype(jnp.int32)[None], pinned(features), pinned(degrees.reshape(ROWS, T)))

    low = move(low, lambda b, r: (b + 4 * r, r))
    high = move(high, lambda b, r: (b + 4 * column(r), column(r)))
    (held,) = call(
        load_kernel, [(edges.shape, BF16)], [HBM], [pltpu.SemaphoreType.DMA], 0, 12 << 20
    )(pinned(edges))
    low, held, meta = lax.optimization_barrier((low, held, meta))
    far_low, far_high = (move(v, lambda b, r: (b + 2, r)) for v in (low, high))
    near_low = move(low, lambda b, r: (b + 1 + 2 * (b % 2), r))

    work = 2 * ROWS * SLOTS * T * T * T
    (total,) = call(first_kernel, [(tiles, F32)], [SMEM] + [VMEM] * 3, (), work, 3 << 20)(
        meta, held, low, high
    )
    high, total = lax.optimization_barrier((high, total))
    near_high = move(high, lambda b, r: (b + 1 + 2 * (b % 2), r))
    last_low, last_high = swap(far_low, 1), swap(far_high, 1)
    (total,) = call(second_kernel, [(tiles, F32)], [SMEM] + [VMEM] * 4, (), work, 3 << 20)(
        meta, held, far_low, far_high, total
    )
    (parts,) = call(third_kernel, [(tiles, BF16)], [SMEM] + [VMEM] * 6, (), 2 * work, 6 << 20)(
        meta, held, near_low, near_high, last_low, last_high, total
    )
    parts = exchange(parts, REP)

    act, send = call(
        dense_kernel,
        [(cot.shape, BF16), ((ROWS, T + GRAD, T), BF16)],
        [VMEM] * 5,
    )(parts, scale, weight, bias[None], cot)
    got = exchange(send, REP)

    sums = [pltpu.VMEM(tiles, F32)]
    near, mine = call(
        near_sums_kernel,
        [(tiles, BF16), ((NODES + 2 * GRAD, T), BF16)],
        [SMEM, VMEM, VMEM],
        sums,
        2 * work,
        6 << 20,
    )(meta, held, got)
    other = swap(mine, 1)
    near = move(near, lambda b, r: (b - 3 + 2 * (b % 2), r))
    (far,) = call(far_sums_kernel, [(tiles, BF16)], [SMEM, VMEM, VMEM], sums, work, 3 << 20)(
        meta, held, got
    )
    (far,) = call(near_kernel, [(tiles, BF16)], [VMEM] * 2)(far, other)
    far, got, other = lax.optimization_barrier((far, got, other))
    far = move(far, lambda b, r: (b - 2, r))
    (own,) = call(own_sums_kernel, [(tiles, F32)], [SMEM] + [VMEM] * 2, sums, work, 3 << 20)(
        meta, held, got
    )
    (grads,) = call(pair_kernel, [((GRAD, T), F32)], [VMEM] * 2, (), PAIR_FLOPS)(mine, other)
    groups = [swap(grads, bits) for bits in (4, 8, 12)]
    low, high = call(total_kernel, [(half, BF16), (half, BF16)], [VMEM] * 3)(own, near, far)
    sent_low, sent_high = low, high
    low = move(low, lambda b, r: (b - 4 * r, r))
    high = move(high, lambda b, r: (b - 4 * r, r ^ 2))
    anywhere = pl.BlockSpec(memory_space=pl.ANY)
    (grads,) = call(
        group_kernel, [((GRAD, T), F32)], [VMEM] * 4 + [anywhere] * 2, (), GROUP_FLOPS
    )(grads, *groups, sent_low, sent_high)
    for bit in (2, 16):
        grads = grads + swap(grads, bit)
    (send,) = call(gather_kernel, [((ROWS, T + 32, T), BF16)], [VMEM] * 3)(low, high, grads)
    got = exchange(send, REP)
    grad_features, grad_weight, grad_bias = call(
        last_kernel,
        [((T, T), F32), ((T, 2 * T), F32), ((1, 2 * T), F32)],
        [VMEM] * 3,
    )(got, scale, grads)
    return act, grad_weight, grad_bias[0], grad_features


def solution(mesh):
    fine = Mesh(mesh.devices.reshape(Z, YL, CORE, X, YH), BLK + REP)
    return jax.shard_map(
        on_device,
        mesh=fine,
        in_specs=(
            P(BLK, None),
            P(BLK),
            P(BLK, REP, None),
            P(BLK, REP),
            P(BLK, REP, None, None, None),
            P(),
            P(),
            P(BLK + REP, None),
        ),
        out_specs=(P(BLK + REP, None), P(), P(), P(BLK + REP, None)),
        check_vma=False,
    )
```

```python
import functools

import jax
import jax.numpy as jnp
from jax import lax
from jax.experimental import pallas as pl
from jax.experimental.pallas import tpu as pltpu
from jax.sharding import Mesh
from jax.sharding import PartitionSpec as P

Z, YL, CORE, X, YH = 8, 2, 2, 4, 2
BLK = ("z", "yl", "core")
REP = ("x", "yh")
T = 128
ROWS = 8
STEPS = 4
SLOTS = 6
HALF = ROWS // 2
NODES = ROWS * T
PAIR_FLOPS, GROUP_FLOPS = 5 * 10**9, 2 * 10**10
GRAD = 48
F32 = jnp.float32
BF16 = jnp.bfloat16

VMEM = pl.BlockSpec(memory_space=pltpu.VMEM)
SMEM = pl.BlockSpec(memory_space=pltpu.SMEM)
HBM = pl.BlockSpec(memory_space=pltpu.HBM)
PARAMS = pltpu.CompilerParams(vmem_limit_bytes=32 * 1024 * 1024)


def bias_rows(total):
    high = total.astype(BF16)
    low = (total - high.astype(F32)).astype(BF16)
    return jnp.concatenate([high, low, jnp.zeros((12, T), BF16)], axis=0)


def prologue_kernel(rep, features, degrees, low, high, scale):
    rows = jnp.concatenate([degrees[...].astype(F32), jnp.ones((T - ROWS, T), F32)], axis=0)
    columns = lax.rsqrt(rows.T)
    for j in range(ROWS):
        inv_root = jnp.broadcast_to(columns[:, j : j + 1], (T, T))
        tile = (features[j * T : (j + 1) * T].astype(F32) * inv_root).astype(BF16)
        half = low if j < HALF else high
        half[j % HALF] = tile

        @pl.when(rep[0] == j)
        def _():
            scale[...] = inv_root


def tile_of(low, high):
    def tile_at(col):
        at = lax.rem(col, HALF)
        return jnp.where(col < HALF, low[at], high[at])

    return tile_at


def product(meta, edges, i, s, tile_at):
    picked = []
    for c in range(SLOTS):
        tile = tile_at(meta[c, s, i])
        picked.append(jnp.where(c < meta[6, s, i], tile, jnp.zeros_like(tile)))
    left = jnp.concatenate([edges[i, s, c] for c in range(SLOTS)], axis=1)
    return jnp.dot(left, jnp.concatenate(picked, axis=0), preferred_element_type=F32)


def load_kernel(edges, held, sem):
    copy = pltpu.make_async_copy(edges, held, sem)
    copy.start()
    copy.wait()


def first_kernel(meta, held, low, high, out):
    for i in range(ROWS):
        out[i] = product(meta, held, i, 0, tile_of(low, high))


def second_kernel(meta, held, low, high, total, out):
    for i in range(ROWS):
        out[i] = total[i] + product(meta, held, i, 2, tile_of(low, high))


def third_kernel(meta, held, near_low, near_high, last_low, last_high, total, out):
    odd = meta[7, 0, 0]
    for i in range(ROWS):
        out[i] = (
            total[i]
            + product(meta, held, i, 3 - 2 * odd, tile_of(near_low, near_high))
            + product(meta, held, i, 1 + 2 * odd, tile_of(last_low, last_high))
        ).astype(BF16)


def dense_kernel(parts, scale, weight, bias, cot, act, send):
    total = parts[0].astype(F32)
    for j in range(1, ROWS):
        total += parts[j].astype(F32)
    agg = (scale[...] * total).astype(BF16)
    pre = jnp.dot(agg, weight[...], preferred_element_type=F32) + bias[...]
    sigma = jax.nn.sigmoid(pre)
    act[...] = (pre * sigma).astype(BF16)
    grad_pre = cot[...].astype(F32) * sigma * (1.0 + pre * (1.0 - sigma))
    half = grad_pre.astype(BF16)
    grad_w = lax.dot_general(agg, half, (((0,), (0,)), ((), ())), preferred_element_type=F32)
    grad_b = jnp.sum(grad_pre, axis=0, keepdims=True)
    grad_b = jnp.concatenate([grad_b[:, :T], grad_b[:, T:]], axis=0)
    back = lax.dot_general(
        half, weight[...], (((1,), (1,)), ((), ())), preferred_element_type=F32
    )
    back = (scale[...] * back).astype(BF16)
    rows_b = bias_rows(grad_b)
    grad_w = grad_w.astype(BF16)
    for j in range(ROWS):
        send[j, 0:T] = back
        send[j, T : T + 16] = grad_w[16 * j : 16 * j + 16, :T]
        send[j, T + 16 : T + 32] = grad_w[16 * j : 16 * j + 16, T:]
        send[j, T + 32 : T + 48] = rows_b


def column_sums(meta, held, got, s, sums):
    sums[...] = jnp.zeros_like(sums)
    for i in range(ROWS):
        back = got[i, 0:T].T
        right = jnp.concatenate([held[i, s, c] for c in range(SLOTS)], axis=1)
        prod = jnp.dot(back, right, preferred_element_type=F32)
        for c in range(SLOTS):
            part = prod[:, c * T : (c + 1) * T]
            at = meta[c, s, i]
            sums[at] += jnp.where(c < meta[6, s, i], part, jnp.zeros_like(part))


def near_sums_kernel(meta, held, got, near, last, sums):
    total = got[0, T:].astype(F32)
    for j in range(1, ROWS):
        total += got[j, T:].astype(F32)
    total = jnp.concatenate(
        [total[0:32], total[32:34] + total[34:36], jnp.zeros((14, T), F32)], axis=0
    )
    high = total.astype(BF16)
    last[NODES : NODES + GRAD] = high
    last[NODES + GRAD :] = (total - high.astype(F32)).astype(BF16)
    column_sums(meta, held, got, 1 + 2 * meta[7, 0, 0], sums)
    last[0:NODES] = sums[...].astype(BF16).reshape(NODES, T)
    column_sums(meta, held, got, 3 - 2 * meta[7, 0, 0], sums)
    near[...] = sums[...].astype(BF16)


def far_sums_kernel(meta, held, got, far, sums):
    column_sums(meta, held, got, 2, sums)
    far[...] = sums[...].astype(BF16)


def own_sums_kernel(meta, held, got, out, sums):
    column_sums(meta, held, got, 0, sums)
    out[...] = sums[...]


def grads_of(rows):
    return rows[NODES : NODES + GRAD].astype(F32) + rows[NODES + GRAD :].astype(F32)


def near_kernel(far, other, out):
    for j in range(ROWS):
        rows = other[j * T : (j + 1) * T].astype(F32)
        out[j] = (far[j].astype(F32) + rows).astype(BF16)


def pair_kernel(mine, other, grads):
    grads[...] = grads_of(mine) + grads_of(other)


def group_kernel(grads, one, two, three, low, high, out):
    out[...] = (grads[...] + one[...]) + (two[...] + three[...])


def total_kernel(own, near, far, low, high):
    for half, first in ((low, 0), (high, HALF)):
        rows = pl.ds(first, HALF)
        total = own[rows] + near[rows].astype(F32) + far[rows].astype(F32)
        half[...] = total.astype(BF16)


def gather_kernel(low, high, grads, out):
    mine = grads[0:32].astype(BF16)
    for j in range(ROWS):
        out[j, 0:T] = low[j] if j < HALF else high[j - HALF]
        out[j, T:] = mine


def last_kernel(got, scale, grads, grad_features, grad_weight, grad_bias):
    total = got[0, 0:T].astype(F32)
    for j in range(1, ROWS):
        total += got[j, 0:T].astype(F32)
    grad_features[...] = scale[...] * total.T
    for j in range(ROWS):
        rows = slice(16 * j, 16 * j + 16)
        grad_weight[rows, :T] = got[j, T : T + 16].astype(F32)
        grad_weight[rows, T:] = got[j, T + 16 :].astype(F32)
    grad_bias[...] = jnp.concatenate([grads[32:33], grads[33:34]], axis=1)


def call(kernel, out, in_specs, scratch=(), flops=0, moved=1 << 20):
    return pl.pallas_call(
        kernel,
        out_shape=[jax.ShapeDtypeStruct(*o) for o in out],
        in_specs=in_specs,
        out_specs=[VMEM] * len(out),
        scratch_shapes=list(scratch),
        cost_estimate=pl.CostEstimate(flops=flops, bytes_accessed=moved, transcendentals=0),
        compiler_params=PARAMS,
    )


def pinned(value):
    return pltpu.with_memory_space_constraint(value, pltpu.HBM)


def exchange(value, axes):
    return lax.all_to_all(value, axes, 0, 0, tiled=True)


def move(value, to):
    blk, rep = Z * YL * CORE, X * YH
    pairs = []
    for b in range(blk):
        for r in range(rep):
            to_b, to_r = to(b, r)
            pairs.append((b * rep + r, to_b % blk * rep + to_r % rep))
    return lax.ppermute(value, BLK + REP, pairs)


def column(r):
    return r ^ (6 if r % 2 else 2)


def far_out(b, r):
    return (b + 2, r) if b % 4 < 2 else (b - 2, r - 1)


def far_back(b, r):
    return (b - 2, r) if b % 4 >= 2 else (b + 2, r + 1)


def swap(value, bit):
    return move(value, lambda b, r: (b ^ bit, r))


def on_device(features, degrees, cols, counts, edges, weight, bias, cot):
    z, yl, core = (lax.axis_index(a) for a in BLK)
    rep = lax.axis_index(REP)
    place = lax.broadcasted_iota(jnp.int32, (1, STEPS, ROWS), 2)
    place = jnp.where(place == 0, core, 0)
    meta = jnp.concatenate([cols.transpose(2, 1, 0), counts.T[None], place], axis=0)

    tiles, half = (ROWS, T, T), (HALF, T, T)
    low, high, scale = call(
        prologue_kernel,
        [(half, BF16), (half, BF16), ((T, T), F32)],
        [SMEM, VMEM, VMEM],
    )(rep.astype(jnp.int32)[None], pinned(features), pinned(degrees.reshape(ROWS, T)))

    low = move(low, lambda b, r: (b + 4 * r, r))
    high = move(high, lambda b, r: (b + 4 * column(r), column(r)))
    (held,) = call(
        load_kernel, [(edges.shape, BF16)], [HBM], [pltpu.SemaphoreType.DMA], 0, 12 << 20
    )(pinned(edges))
    low, held, meta = lax.optimization_barrier((low, held, meta))
    far_low, far_high = (move(v, far_out) for v in (low, high))
    near_low = move(low, lambda b, r: (b + 1 + 2 * (b % 2), r))

    work = 2 * ROWS * SLOTS * T * T * T
    (total,) = call(first_kernel, [(tiles, F32)], [SMEM] + [VMEM] * 3, (), work, 3 << 20)(
        meta, held, low, high
    )
    high, total = lax.optimization_barrier((high, total))
    near_high = move(high, lambda b, r: (b + 1 + 2 * (b % 2), r))
    last_low, last_high = swap(far_low, 1), swap(far_high, 1)
    (total,) = call(second_kernel, [(tiles, F32)], [SMEM] + [VMEM] * 4, (), work, 3 << 20)(
        meta, held, far_low, far_high, total
    )
    (parts,) = call(third_kernel, [(tiles, BF16)], [SMEM] + [VMEM] * 6, (), 2 * work, 6 << 20)(
        meta, held, near_low, near_high, last_low, last_high, total
    )
    parts = exchange(parts, REP)

    act, send = call(
        dense_kernel,
        [(cot.shape, BF16), ((ROWS, T + GRAD, T), BF16)],
        [VMEM] * 5,
    )(parts, scale, weight, bias[None], cot)
    got = exchange(send, REP)

    sums = [pltpu.VMEM(tiles, F32)]
    near, mine = call(
        near_sums_kernel,
        [(tiles, BF16), ((NODES + 2 * GRAD, T), BF16)],
        [SMEM, VMEM, VMEM],
        sums,
        2 * work,
        6 << 20,
    )(meta, held, got)
    other = swap(mine, 1)
    near = move(near, lambda b, r: (b - 3 + 2 * (b % 2), r))
    (far,) = call(far_sums_kernel, [(tiles, BF16)], [SMEM, VMEM, VMEM], sums, work, 3 << 20)(
        meta, held, got
    )
    (far,) = call(near_kernel, [(tiles, BF16)], [VMEM] * 2)(far, other)
    far, got, other = lax.optimization_barrier((far, got, other))
    far = move(far, far_back)
    (own,) = call(own_sums_kernel, [(tiles, F32)], [SMEM] + [VMEM] * 2, sums, work, 3 << 20)(
        meta, held, got
    )
    (grads,) = call(pair_kernel, [((GRAD, T), F32)], [VMEM] * 2, (), PAIR_FLOPS)(mine, other)
    groups = [swap(grads, bits) for bits in (4, 8, 12)]
    low, high = call(total_kernel, [(half, BF16), (half, BF16)], [VMEM] * 3)(own, near, far)
    sent_low, sent_high = low, high
    low = move(low, lambda b, r: (b - 4 * r, r))
    high = move(high, lambda b, r: (b - 4 * r, r ^ 2))
    anywhere = pl.BlockSpec(memory_space=pl.ANY)
    (grads,) = call(
        group_kernel, [((GRAD, T), F32)], [VMEM] * 4 + [anywhere] * 2, (), GROUP_FLOPS
    )(grads, *groups, sent_low, sent_high)
    for bit in (2, 16):
        grads = grads + swap(grads, bit)
    (send,) = call(gather_kernel, [((ROWS, T + 32, T), BF16)], [VMEM] * 3)(low, high, grads)
    got = exchange(send, REP)
    grad_features, grad_weight, grad_bias = call(
        last_kernel,
        [((T, T), F32), ((T, 2 * T), F32), ((1, 2 * T), F32)],
        [VMEM] * 3,
    )(got, scale, grads)
    return act, grad_weight, grad_bias[0], grad_features


def solution(mesh):
    fine = Mesh(mesh.devices.reshape(Z, YL, CORE, X, YH), BLK + REP)
    return jax.shard_map(
        on_device,
        mesh=fine,
        in_specs=(
            P(BLK, None),
            P(BLK),
            P(BLK, REP, None),
            P(BLK, REP),
            P(BLK, REP, None, None, None),
            P(),
            P(),
            P(BLK + REP, None),
        ),
        out_specs=(P(BLK + REP, None), P(), P(), P(BLK + REP, None)),
        check_vma=False,
    )
```

```python
import functools

import jax
import jax.numpy as jnp
from jax import lax
from jax.experimental import pallas as pl
from jax.experimental.pallas import tpu as pltpu
from jax.sharding import Mesh
from jax.sharding import PartitionSpec as P

Z, YL, CORE, X, YH = 8, 2, 2, 4, 2
BLK = ("z", "yl", "core")
REP = ("x", "yh")
T = 128
ROWS = 8
STEPS = 4
SLOTS = 6
HALF = ROWS // 2
NODES = ROWS * T
PAIR_FLOPS, GROUP_FLOPS = 5 * 10**9, 2 * 10**10
GRAD = 48
F32 = jnp.float32
BF16 = jnp.bfloat16

VMEM = pl.BlockSpec(memory_space=pltpu.VMEM)
SMEM = pl.BlockSpec(memory_space=pltpu.SMEM)
HBM = pl.BlockSpec(memory_space=pltpu.HBM)
PARAMS = pltpu.CompilerParams(vmem_limit_bytes=32 * 1024 * 1024)


def bias_rows(total):
    high = total.astype(BF16)
    low = (total - high.astype(F32)).astype(BF16)
    return jnp.concatenate([high, low, jnp.zeros((12, T), BF16)], axis=0)


def prologue_kernel(rep, features, degrees, low, high, scale):
    rows = jnp.concatenate([degrees[...].astype(F32), jnp.ones((T - ROWS, T), F32)], axis=0)
    columns = lax.rsqrt(rows.T)
    for j in range(ROWS):
        inv_root = jnp.broadcast_to(columns[:, j : j + 1], (T, T))
        tile = (features[j * T : (j + 1) * T].astype(F32) * inv_root).astype(BF16)
        half = low if j < HALF else high
        half[j % HALF] = tile

        @pl.when(rep[0] == j)
        def _():
            scale[...] = inv_root


def fill(tiles, low, high):
    tiles[0:HALF] = low[...]
    tiles[HALF:ROWS] = high[...]
    tiles[ROWS] = jnp.zeros((T, T), BF16)


def tile_id(meta, i, s, c):
    return jnp.where(c < meta[6, s, i], meta[c, s, i], ROWS)


def product(meta, edges, i, s, tiles):
    picked = [tiles[tile_id(meta, i, s, c)] for c in range(SLOTS)]
    left = jnp.concatenate([edges[i, s, c] for c in range(SLOTS)], axis=1)
    return jnp.dot(left, jnp.concatenate(picked, axis=0), preferred_element_type=F32)


def load_kernel(edges, held, sem):
    copy = pltpu.make_async_copy(edges, held, sem)
    copy.start()
    copy.wait()


def first_kernel(meta, held, low, high, out, tiles):
    fill(tiles, low, high)
    for i in range(ROWS):
        out[i] = product(meta, held, i, 0, tiles)


def second_kernel(meta, held, low, high, total, out, tiles):
    fill(tiles, low, high)
    for i in range(ROWS):
        out[i] = total[i] + product(meta, held, i, 2, tiles)


def third_kernel(meta, held, near_low, near_high, last_low, last_high, total, out, near, last):
    odd = meta[7, 0, 0]
    fill(near, near_low, near_high)
    fill(last, last_low, last_high)
    for i in range(ROWS):
        out[i] = (
            total[i]
            + product(meta, held, i, 3 - 2 * odd, near)
            + product(meta, held, i, 1 + 2 * odd, last)
        ).astype(BF16)


def dense_kernel(parts, scale, weight, bias, cot, act, send):
    total = parts[0].astype(F32)
    for j in range(1, ROWS):
        total += parts[j].astype(F32)
    agg = (scale[...] * total).astype(BF16)
    pre = jnp.dot(agg, weight[...], preferred_element_type=F32) + bias[...]
    sigma = jax.nn.sigmoid(pre)
    act[...] = (pre * sigma).astype(BF16)
    grad_pre = cot[...].astype(F32) * sigma * (1.0 + pre * (1.0 - sigma))
    half = grad_pre.astype(BF16)
    grad_w = lax.dot_general(agg, half, (((0,), (0,)), ((), ())), preferred_element_type=F32)
    grad_b = jnp.sum(grad_pre, axis=0, keepdims=True)
    grad_b = jnp.concatenate([grad_b[:, :T], grad_b[:, T:]], axis=0)
    back = lax.dot_general(
        half, weight[...], (((1,), (1,)), ((), ())), preferred_element_type=F32
    )
    back = (scale[...] * back).astype(BF16)
    rows_b = bias_rows(grad_b)
    grad_w = grad_w.astype(BF16)
    for j in range(ROWS):
        send[j, 0:T] = back
        send[j, T : T + 16] = grad_w[16 * j : 16 * j + 16, :T]
        send[j, T + 16 : T + 32] = grad_w[16 * j : 16 * j + 16, T:]
        send[j, T + 32 : T + 48] = rows_b


def column_sums(meta, held, got, s, sums):
    sums[...] = jnp.zeros_like(sums)
    for i in range(ROWS):
        back = got[i, 0:T].T
        right = jnp.concatenate([held[i, s, c] for c in range(SLOTS)], axis=1)
        prod = jnp.dot(back, right, preferred_element_type=F32)
        for c in range(SLOTS):
            part = prod[:, c * T : (c + 1) * T]
            sums[tile_id(meta, i, s, c)] += part


def near_sums_kernel(meta, held, got, near, last, sums):
    total = got[0, T:].astype(F32)
    for j in range(1, ROWS):
        total += got[j, T:].astype(F32)
    total = jnp.concatenate(
        [total[0:32], total[32:34] + total[34:36], jnp.zeros((14, T), F32)], axis=0
    )
    high = total.astype(BF16)
    last[NODES : NODES + GRAD] = high
    last[NODES + GRAD :] = (total - high.astype(F32)).astype(BF16)
    column_sums(meta, held, got, 1 + 2 * meta[7, 0, 0], sums)
    last[0:NODES] = sums[0:ROWS].astype(BF16).reshape(NODES, T)
    column_sums(meta, held, got, 3 - 2 * meta[7, 0, 0], sums)
    near[...] = sums[0:ROWS].astype(BF16)


def far_sums_kernel(meta, held, got, far, sums):
    column_sums(meta, held, got, 2, sums)
    far[...] = sums[0:ROWS].astype(BF16)


def own_sums_kernel(meta, held, got, out, sums):
    column_sums(meta, held, got, 0, sums)
    out[...] = sums[0:ROWS]


def grads_of(rows):
    return rows[NODES : NODES + GRAD].astype(F32) + rows[NODES + GRAD :].astype(F32)


def near_kernel(far, other, out):
    for j in range(ROWS):
        rows = other[j * T : (j + 1) * T].astype(F32)
        out[j] = (far[j].astype(F32) + rows).astype(BF16)


def pair_kernel(mine, other, grads):
    grads[...] = grads_of(mine) + grads_of(other)


def group_kernel(grads, one, two, three, low, high, out):
    out[...] = (grads[...] + one[...]) + (two[...] + three[...])


def total_kernel(own, near, far, low, high):
    for half, first in ((low, 0), (high, HALF)):
        rows = pl.ds(first, HALF)
        total = own[rows] + near[rows].astype(F32) + far[rows].astype(F32)
        half[...] = total.astype(BF16)


def gather_kernel(low, high, grads, out):
    mine = grads[0:32].astype(BF16)
    for j in range(ROWS):
        out[j, 0:T] = low[j] if j < HALF else high[j - HALF]
        out[j, T:] = mine


def last_kernel(got, scale, grads, grad_features, grad_weight, grad_bias):
    total = got[0, 0:T].astype(F32)
    for j in range(1, ROWS):
        total += got[j, 0:T].astype(F32)
    grad_features[...] = scale[...] * total.T
    for j in range(ROWS):
        rows = slice(16 * j, 16 * j + 16)
        grad_weight[rows, :T] = got[j, T : T + 16].astype(F32)
        grad_weight[rows, T:] = got[j, T + 16 :].astype(F32)
    grad_bias[...] = jnp.concatenate([grads[32:33], grads[33:34]], axis=1)


def call(kernel, out, in_specs, scratch=(), flops=0, moved=1 << 20):
    return pl.pallas_call(
        kernel,
        out_shape=[jax.ShapeDtypeStruct(*o) for o in out],
        in_specs=in_specs,
        out_specs=[VMEM] * len(out),
        scratch_shapes=list(scratch),
        cost_estimate=pl.CostEstimate(flops=flops, bytes_accessed=moved, transcendentals=0),
        compiler_params=PARAMS,
    )


def pinned(value):
    return pltpu.with_memory_space_constraint(value, pltpu.HBM)


def exchange(value, axes):
    return lax.all_to_all(value, axes, 0, 0, tiled=True)


def move(value, to):
    blk, rep = Z * YL * CORE, X * YH
    pairs = []
    for b in range(blk):
        for r in range(rep):
            to_b, to_r = to(b, r)
            pairs.append((b * rep + r, to_b % blk * rep + to_r % rep))
    return lax.ppermute(value, BLK + REP, pairs)


def column(r):
    return r ^ (6 if r % 2 else 2)


def far_out(b, r):
    return (b + 2, r) if b % 4 < 2 else (b - 2, r - 1)


def far_back(b, r):
    return (b - 2, r) if b % 4 >= 2 else (b + 2, r + 1)


def swap(value, bit):
    return move(value, lambda b, r: (b ^ bit, r))


def on_device(features, degrees, cols, counts, edges, weight, bias, cot):
    z, yl, core = (lax.axis_index(a) for a in BLK)
    rep = lax.axis_index(REP)
    place = lax.broadcasted_iota(jnp.int32, (1, STEPS, ROWS), 2)
    place = jnp.where(place == 0, core, 0)
    meta = jnp.concatenate([cols.transpose(2, 1, 0), counts.T[None], place], axis=0)

    tiles, half = (ROWS, T, T), (HALF, T, T)
    low, high, scale = call(
        prologue_kernel,
        [(half, BF16), (half, BF16), ((T, T), F32)],
        [SMEM, VMEM, VMEM],
    )(rep.astype(jnp.int32)[None], pinned(features), pinned(degrees.reshape(ROWS, T)))

    low = move(low, lambda b, r: (b + 4 * r, r))
    high = move(high, lambda b, r: (b + 4 * column(r), column(r)))
    (held,) = call(
        load_kernel, [(edges.shape, BF16)], [HBM], [pltpu.SemaphoreType.DMA], 0, 12 << 20
    )(pinned(edges))
    low, held, meta = lax.optimization_barrier((low, held, meta))
    far_low, far_high = (move(v, far_out) for v in (low, high))
    near_low = move(low, lambda b, r: (b + 1 + 2 * (b % 2), r))

    work = 2 * ROWS * SLOTS * T * T * T
    block = pltpu.VMEM((ROWS + 1, T, T), BF16)
    (total,) = call(first_kernel, [(tiles, F32)], [SMEM] + [VMEM] * 3, [block], work, 3 << 20)(
        meta, held, low, high
    )
    high, total = lax.optimization_barrier((high, total))
    near_high = move(high, lambda b, r: (b + 1 + 2 * (b % 2), r))
    last_low, last_high = swap(far_low, 1), swap(far_high, 1)
    (total,) = call(second_kernel, [(tiles, F32)], [SMEM] + [VMEM] * 4, [block], work, 3 << 20)(
        meta, held, far_low, far_high, total
    )
    (parts,) = call(third_kernel, [(tiles, BF16)], [SMEM] + [VMEM] * 6, [block] * 2, 2 * work, 6 << 20)(
        meta, held, near_low, near_high, last_low, last_high, total
    )
    parts = exchange(parts, REP)

    act, send = call(
        dense_kernel,
        [(cot.shape, BF16), ((ROWS, T + GRAD, T), BF16)],
        [VMEM] * 5,
    )(parts, scale, weight, bias[None], cot)
    got = exchange(send, REP)

    sums = [pltpu.VMEM((ROWS + 1, T, T), F32)]
    near, mine = call(
        near_sums_kernel,
        [(tiles, BF16), ((NODES + 2 * GRAD, T), BF16)],
        [SMEM, VMEM, VMEM],
        sums,
        2 * work,
        6 << 20,
    )(meta, held, got)
    other = swap(mine, 1)
    near = move(near, lambda b, r: (b - 3 + 2 * (b % 2), r))
    (far,) = call(far_sums_kernel, [(tiles, BF16)], [SMEM, VMEM, VMEM], sums, work, 3 << 20)(
        meta, held, got
    )
    (far,) = call(near_kernel, [(tiles, BF16)], [VMEM] * 2)(far, other)
    far, got, other = lax.optimization_barrier((far, got, other))
    far = move(far, far_back)
    (own,) = call(own_sums_kernel, [(tiles, F32)], [SMEM] + [VMEM] * 2, sums, work, 3 << 20)(
        meta, held, got
    )
    (grads,) = call(pair_kernel, [((GRAD, T), F32)], [VMEM] * 2, (), PAIR_FLOPS)(mine, other)
    groups = [swap(grads, bits) for bits in (4, 8, 12)]
    low, high = call(total_kernel, [(half, BF16), (half, BF16)], [VMEM] * 3)(own, near, far)
    sent_low, sent_high = low, high
    low = move(low, lambda b, r: (b - 4 * r, r))
    high = move(high, lambda b, r: (b - 4 * r, r ^ 2))
    anywhere = pl.BlockSpec(memory_space=pl.ANY)
    (grads,) = call(
        group_kernel, [((GRAD, T), F32)], [VMEM] * 4 + [anywhere] * 2, (), GROUP_FLOPS
    )(grads, *groups, sent_low, sent_high)
    for bit in (2, 16):
        grads = grads + swap(grads, bit)
    (send,) = call(gather_kernel, [((ROWS, T + 32, T), BF16)], [VMEM] * 3)(low, high, grads)
    got = exchange(send, REP)
    grad_features, grad_weight, grad_bias = call(
        last_kernel,
        [((T, T), F32), ((T, 2 * T), F32), ((1, 2 * T), F32)],
        [VMEM] * 3,
    )(got, scale, grads)
    return act, grad_weight, grad_bias[0], grad_features


def solution(mesh):
    fine = Mesh(mesh.devices.reshape(Z, YL, CORE, X, YH), BLK + REP)
    return jax.shard_map(
        on_device,
        mesh=fine,
        in_specs=(
            P(BLK, None),
            P(BLK),
            P(BLK, REP, None),
            P(BLK, REP),
            P(BLK, REP, None, None, None),
            P(),
            P(),
            P(BLK + REP, None),
        ),
        out_specs=(P(BLK + REP, None), P(), P(), P(BLK + REP, None)),
        check_vma=False,
    )
```

```python
import functools

import jax
import jax.numpy as jnp
from jax import lax
from jax.experimental import pallas as pl
from jax.experimental.pallas import tpu as pltpu
from jax.sharding import Mesh
from jax.sharding import PartitionSpec as P

Z, YL, CORE, X, YH = 8, 2, 2, 4, 2
BLK = ("z", "yl", "core")
REP = ("x", "yh")
T = 128
ROWS = 8
STEPS = 4
SLOTS = 6
HALF = ROWS // 2
NODES = ROWS * T
PAIR_FLOPS, GROUP_FLOPS = 5 * 10**9, 2 * 10**10
GRAD = 48
F32 = jnp.float32
BF16 = jnp.bfloat16

VMEM = pl.BlockSpec(memory_space=pltpu.VMEM)
SMEM = pl.BlockSpec(memory_space=pltpu.SMEM)
HBM = pl.BlockSpec(memory_space=pltpu.HBM)
PARAMS = pltpu.CompilerParams(vmem_limit_bytes=32 * 1024 * 1024)


def bias_rows(total):
    high = total.astype(BF16)
    low = (total - high.astype(F32)).astype(BF16)
    return jnp.concatenate([high, low, jnp.zeros((12, T), BF16)], axis=0)


def prologue_kernel(rep, features, degrees, low, high, scale):
    rows = jnp.concatenate([degrees[...].astype(F32), jnp.ones((T - ROWS, T), F32)], axis=0)
    columns = lax.rsqrt(rows.T)
    for j in range(ROWS):
        inv_root = jnp.broadcast_to(columns[:, j : j + 1], (T, T))
        tile = (features[j * T : (j + 1) * T].astype(F32) * inv_root).astype(BF16)
        half = low if j < HALF else high
        half[j % HALF] = tile

        @pl.when(rep[0] == j)
        def _():
            scale[...] = inv_root


def fill(tiles, low, high):
    tiles[0:HALF] = low[...]
    tiles[HALF:ROWS] = high[...]
    tiles[ROWS] = jnp.zeros((T, T), BF16)


def tile_id(meta, i, s, c):
    return jnp.where(c < meta[6, s, i], meta[c, s, i], ROWS)


def product(meta, edges, i, s, tiles):
    picked = [tiles[tile_id(meta, i, s, c)] for c in range(SLOTS)]
    left = jnp.concatenate([edges[i, s, c] for c in range(SLOTS)], axis=1)
    return jnp.dot(left, jnp.concatenate(picked, axis=0), preferred_element_type=F32)


def load_kernel(edges, held, sem):
    copy = pltpu.make_async_copy(edges, held, sem)
    copy.start()
    copy.wait()


def first_kernel(meta, held, low, high, out, tiles):
    fill(tiles, low, high)
    for i in range(ROWS):
        out[i] = product(meta, held, i, 0, tiles)


def second_kernel(meta, held, low, high, total, out, tiles):
    fill(tiles, low, high)
    for i in range(ROWS):
        out[i] = total[i] + product(meta, held, i, 2, tiles)


def third_kernel(meta, held, near_low, near_high, last_low, last_high, total, out, near, last):
    odd = meta[7, 0, 0]
    fill(near, near_low, near_high)
    fill(last, last_low, last_high)
    for i in range(ROWS):
        out[i] = (
            total[i]
            + product(meta, held, i, 3 - 2 * odd, near)
            + product(meta, held, i, 1 + 2 * odd, last)
        ).astype(BF16)


def dense_kernel(parts, scale, weight, bias, cot, act, send):
    total = parts[0].astype(F32)
    for j in range(1, ROWS):
        total += parts[j].astype(F32)
    agg = (scale[...] * total).astype(BF16)
    pre = jnp.dot(agg, weight[...], preferred_element_type=F32) + bias[...]
    sigma = jax.nn.sigmoid(pre)
    act[...] = (pre * sigma).astype(BF16)
    grad_pre = cot[...].astype(F32) * sigma * (1.0 + pre * (1.0 - sigma))
    half = grad_pre.astype(BF16)
    grad_w = lax.dot_general(agg, half, (((0,), (0,)), ((), ())), preferred_element_type=F32)
    grad_b = jnp.sum(grad_pre, axis=0, keepdims=True)
    grad_b = jnp.concatenate([grad_b[:, :T], grad_b[:, T:]], axis=0)
    back = lax.dot_general(
        half, weight[...], (((1,), (1,)), ((), ())), preferred_element_type=F32
    )
    back = (scale[...] * back).astype(BF16)
    rows_b = bias_rows(grad_b)
    grad_w = grad_w.astype(BF16)
    for j in range(ROWS):
        send[j, 0:T] = back
        send[j, T : T + 16] = grad_w[16 * j : 16 * j + 16, :T]
        send[j, T + 16 : T + 32] = grad_w[16 * j : 16 * j + 16, T:]
        send[j, T + 32 : T + 48] = rows_b


def column_sums(meta, held, got, s, sums):
    sums[...] = jnp.zeros_like(sums)
    for i in range(ROWS):
        back = got[i, 0:T].T
        right = jnp.concatenate([held[i, s, c] for c in range(SLOTS)], axis=1)
        prod = jnp.dot(back, right, preferred_element_type=F32)
        for c in range(SLOTS):
            part = prod[:, c * T : (c + 1) * T]
            sums[tile_id(meta, i, s, c)] += part


def near_sums_kernel(meta, held, got, near, last, sums):
    total = got[0, T:].astype(F32)
    for j in range(1, ROWS):
        total += got[j, T:].astype(F32)
    total = jnp.concatenate(
        [total[0:32], total[32:34] + total[34:36], jnp.zeros((14, T), F32)], axis=0
    )
    high = total.astype(BF16)
    last[NODES : NODES + GRAD] = high
    last[NODES + GRAD :] = (total - high.astype(F32)).astype(BF16)
    column_sums(meta, held, got, 1 + 2 * meta[7, 0, 0], sums)
    last[0:NODES] = sums[0:ROWS].astype(BF16).reshape(NODES, T)
    column_sums(meta, held, got, 3 - 2 * meta[7, 0, 0], sums)
    near[...] = sums[0:ROWS].astype(BF16)


def far_sums_kernel(meta, held, got, far, sums):
    column_sums(meta, held, got, 2, sums)
    far[...] = sums[0:ROWS].astype(BF16)


def own_sums_kernel(meta, held, got, out, sums):
    column_sums(meta, held, got, 0, sums)
    out[...] = sums[0:ROWS]


def grads_of(rows):
    return rows[NODES : NODES + GRAD].astype(F32) + rows[NODES + GRAD :].astype(F32)


def near_kernel(far, other, out):
    for j in range(ROWS):
        rows = other[j * T : (j + 1) * T].astype(F32)
        out[j] = (far[j].astype(F32) + rows).astype(BF16)


def bias_of(rows):
    return rows[32:34].astype(F32) + rows[34:36].astype(F32)


def slice_rows(weights, bias):
    return jnp.concatenate([weights.astype(BF16), bias_rows(bias)], axis=0)


def pair_kernel(mine, other, grads):
    total = grads_of(mine) + grads_of(other)
    grads[...] = slice_rows(total[0:32], total[32:34])


def group_kernel(grads, one, two, three, low, high, out):
    a, b, c, d = (v[0:32].astype(F32) for v in (grads, one, two, three))
    bias = (bias_of(grads) + bias_of(one)) + (bias_of(two) + bias_of(three))
    out[...] = slice_rows((a + b) + (c + d), bias)


def add_kernel(grads, other, out):
    total = grads[0:32].astype(F32) + other[0:32].astype(F32)
    out[...] = slice_rows(total, bias_of(grads) + bias_of(other))


def total_kernel(own, near, far, low, high):
    for half, first in ((low, 0), (high, HALF)):
        rows = pl.ds(first, HALF)
        total = own[rows] + near[rows].astype(F32) + far[rows].astype(F32)
        half[...] = total.astype(BF16)


def gather_kernel(low, high, grads, out):
    mine = grads[0:32]
    for j in range(ROWS):
        out[j, 0:T] = low[j] if j < HALF else high[j - HALF]
        out[j, T:] = mine


def last_kernel(got, scale, grads, grad_features, grad_weight, grad_bias):
    total = got[0, 0:T].astype(F32)
    for j in range(1, ROWS):
        total += got[j, 0:T].astype(F32)
    grad_features[...] = scale[...] * total.T
    for j in range(ROWS):
        rows = slice(16 * j, 16 * j + 16)
        grad_weight[rows, :T] = got[j, T : T + 16].astype(F32)
        grad_weight[rows, T:] = got[j, T + 16 :].astype(F32)
    bias = bias_of(grads)
    grad_bias[...] = jnp.concatenate([bias[0:1], bias[1:2]], axis=1)


def call(kernel, out, in_specs, scratch=(), flops=0, moved=1 << 20):
    return pl.pallas_call(
        kernel,
        out_shape=[jax.ShapeDtypeStruct(*o) for o in out],
        in_specs=in_specs,
        out_specs=[VMEM] * len(out),
        scratch_shapes=list(scratch),
        cost_estimate=pl.CostEstimate(flops=flops, bytes_accessed=moved, transcendentals=0),
        compiler_params=PARAMS,
    )


def pinned(value):
    return pltpu.with_memory_space_constraint(value, pltpu.HBM)


def exchange(value, axes):
    return lax.all_to_all(value, axes, 0, 0, tiled=True)


def move(value, to):
    blk, rep = Z * YL * CORE, X * YH
    pairs = []
    for b in range(blk):
        for r in range(rep):
            to_b, to_r = to(b, r)
            pairs.append((b * rep + r, to_b % blk * rep + to_r % rep))
    return lax.ppermute(value, BLK + REP, pairs)


def column(r):
    return r ^ (6 if r % 2 else 2)


def far_out(b, r):
    return (b + 2, r) if b % 4 < 2 else (b - 2, r - 1)


def far_back(b, r):
    return (b - 2, r) if b % 4 >= 2 else (b + 2, r + 1)


def swap(value, bit):
    return move(value, lambda b, r: (b ^ bit, r))


def on_device(features, degrees, cols, counts, edges, weight, bias, cot):
    z, yl, core = (lax.axis_index(a) for a in BLK)
    rep = lax.axis_index(REP)
    place = lax.broadcasted_iota(jnp.int32, (1, STEPS, ROWS), 2)
    place = jnp.where(place == 0, core, 0)
    meta = jnp.concatenate([cols.transpose(2, 1, 0), counts.T[None], place], axis=0)

    tiles, half = (ROWS, T, T), (HALF, T, T)
    low, high, scale = call(
        prologue_kernel,
        [(half, BF16), (half, BF16), ((T, T), F32)],
        [SMEM, VMEM, VMEM],
    )(rep.astype(jnp.int32)[None], pinned(features), pinned(degrees.reshape(ROWS, T)))

    low = move(low, lambda b, r: (b + 4 * r, r))
    high = move(high, lambda b, r: (b + 4 * column(r), column(r)))
    (held,) = call(
        load_kernel, [(edges.shape, BF16)], [HBM], [pltpu.SemaphoreType.DMA], 0, 12 << 20
    )(pinned(edges))
    low, held, meta = lax.optimization_barrier((low, held, meta))
    far_low, far_high = (move(v, far_out) for v in (low, high))
    near_low = move(low, lambda b, r: (b + 1 + 2 * (b % 2), r))

    work = 2 * ROWS * SLOTS * T * T * T
    block = pltpu.VMEM((ROWS + 1, T, T), BF16)
    (total,) = call(first_kernel, [(tiles, F32)], [SMEM] + [VMEM] * 3, [block], work, 3 << 20)(
        meta, held, low, high
    )
    high, total = lax.optimization_barrier((high, total))
    near_high = move(high, lambda b, r: (b + 1 + 2 * (b % 2), r))
    last_low, last_high = swap(far_low, 1), swap(far_high, 1)
    (total,) = call(second_kernel, [(tiles, F32)], [SMEM] + [VMEM] * 4, [block], work, 3 << 20)(
        meta, held, far_low, far_high, total
    )
    (parts,) = call(third_kernel, [(tiles, BF16)], [SMEM] + [VMEM] * 6, [block] * 2, 2 * work, 6 << 20)(
        meta, held, near_low, near_high, last_low, last_high, total
    )
    parts = exchange(parts, REP)

    act, send = call(
        dense_kernel,
        [(cot.shape, BF16), ((ROWS, T + GRAD, T), BF16)],
        [VMEM] * 5,
    )(parts, scale, weight, bias[None], cot)
    got = exchange(send, REP)

    sums = [pltpu.VMEM((ROWS + 1, T, T), F32)]
    near, mine = call(
        near_sums_kernel,
        [(tiles, BF16), ((NODES + 2 * GRAD, T), BF16)],
        [SMEM, VMEM, VMEM],
        sums,
        2 * work,
        6 << 20,
    )(meta, held, got)
    other = swap(mine, 1)
    near = move(near, lambda b, r: (b - 3 + 2 * (b % 2), r))
    (far,) = call(far_sums_kernel, [(tiles, BF16)], [SMEM, VMEM, VMEM], sums, work, 3 << 20)(
        meta, held, got
    )
    (far,) = call(near_kernel, [(tiles, BF16)], [VMEM] * 2)(far, other)
    far, got, other = lax.optimization_barrier((far, got, other))
    far = move(far, far_back)
    (own,) = call(own_sums_kernel, [(tiles, F32)], [SMEM] + [VMEM] * 2, sums, work, 3 << 20)(
        meta, held, got
    )
    (grads,) = call(pair_kernel, [((GRAD, T), BF16)], [VMEM] * 2, (), PAIR_FLOPS)(mine, other)
    groups = [swap(grads, bits) for bits in (4, 8, 12)]
    low, high = call(total_kernel, [(half, BF16), (half, BF16)], [VMEM] * 3)(own, near, far)
    sent_low, sent_high = low, high
    low = move(low, lambda b, r: (b - 4 * r, r))
    high = move(high, lambda b, r: (b - 4 * r, r ^ 2))
    anywhere = pl.BlockSpec(memory_space=pl.ANY)
    (grads,) = call(
        group_kernel, [((GRAD, T), BF16)], [VMEM] * 4 + [anywhere] * 2, (), GROUP_FLOPS
    )(grads, *groups, sent_low, sent_high)
    for bit in (2, 16):
        (grads,) = call(add_kernel, [((GRAD, T), BF16)], [VMEM] * 2)(grads, swap(grads, bit))
    (send,) = call(gather_kernel, [((ROWS, T + 32, T), BF16)], [VMEM] * 3)(low, high, grads)
    got = exchange(send, REP)
    grad_features, grad_weight, grad_bias = call(
        last_kernel,
        [((T, T), F32), ((T, 2 * T), F32), ((1, 2 * T), F32)],
        [VMEM] * 3,
    )(got, scale, grads)
    return act, grad_weight, grad_bias[0], grad_features


def solution(mesh):
    fine = Mesh(mesh.devices.reshape(Z, YL, CORE, X, YH), BLK + REP)
    return jax.shard_map(
        on_device,
        mesh=fine,
        in_specs=(
            P(BLK, None),
            P(BLK),
            P(BLK, REP, None),
            P(BLK, REP),
            P(BLK, REP, None, None, None),
            P(),
            P(),
            P(BLK + REP, None),
        ),
        out_specs=(P(BLK + REP, None), P(), P(), P(BLK + REP, None)),
        check_vma=False,
    )
```

```python
import functools

import jax
import jax.numpy as jnp
from jax import lax
from jax.experimental import pallas as pl
from jax.experimental.pallas import tpu as pltpu
from jax.sharding import Mesh
from jax.sharding import PartitionSpec as P

Z, YL, CORE, X, YH = 8, 2, 2, 4, 2
BLK = ("z", "yl", "core")
REP = ("x", "yh")
T = 128
ROWS = 8
STEPS = 4
SLOTS = 6
HALF = ROWS // 2
NODES = ROWS * T
PAIR_FLOPS, GROUP_FLOPS = 5 * 10**9, 2 * 10**10
GRAD = 48
F32 = jnp.float32
BF16 = jnp.bfloat16

VMEM = pl.BlockSpec(memory_space=pltpu.VMEM)
SMEM = pl.BlockSpec(memory_space=pltpu.SMEM)
HBM = pl.BlockSpec(memory_space=pltpu.HBM)
PARAMS = pltpu.CompilerParams(vmem_limit_bytes=32 * 1024 * 1024)


def bias_rows(total):
    high = total.astype(BF16)
    low = (total - high.astype(F32)).astype(BF16)
    return jnp.concatenate([high, low, jnp.zeros((12, T), BF16)], axis=0)


def prologue_kernel(rep, features, degrees, low, high, scale):
    rows = jnp.concatenate([degrees[...].astype(F32), jnp.ones((T - ROWS, T), F32)], axis=0)
    columns = lax.rsqrt(rows.T)
    for j in range(ROWS):
        inv_root = jnp.broadcast_to(columns[:, j : j + 1], (T, T))
        tile = (features[j * T : (j + 1) * T].astype(F32) * inv_root).astype(BF16)
        half = low if j < HALF else high
        half[j % HALF] = tile

        @pl.when(rep[0] == j)
        def _():
            scale[...] = inv_root


def fill(tiles, low, high):
    tiles[0:HALF] = low[...]
    tiles[HALF:ROWS] = high[...]
    tiles[ROWS] = jnp.zeros((T, T), BF16)


def tile_id(meta, i, s, c):
    return jnp.where(c < meta[6, s, i], meta[c, s, i], ROWS)


def product(meta, edges, i, s, tiles):
    picked = [tiles[tile_id(meta, i, s, c)] for c in range(SLOTS)]
    left = jnp.concatenate([edges[i, s, c] for c in range(SLOTS)], axis=1)
    return jnp.dot(left, jnp.concatenate(picked, axis=0), preferred_element_type=F32)


def load_kernel(edges, held, sem):
    copy = pltpu.make_async_copy(edges, held, sem)
    copy.start()
    copy.wait()


def first_kernel(meta, held, low, high, out, tiles):
    fill(tiles, low, high)
    for i in range(ROWS):
        out[i] = product(meta, held, i, 0, tiles)


def second_kernel(meta, held, low, high, total, out, tiles):
    fill(tiles, low, high)
    for i in range(ROWS):
        out[i] = total[i] + product(meta, held, i, 2, tiles)


def third_kernel(meta, held, near_low, near_high, last_low, last_high, total, out, near, last):
    odd = meta[7, 0, 0]
    fill(near, near_low, near_high)
    fill(last, last_low, last_high)
    for i in range(ROWS):
        out[i] = (
            total[i]
            + product(meta, held, i, 3 - 2 * odd, near)
            + product(meta, held, i, 1 + 2 * odd, last)
        ).astype(BF16)


def dense_kernel(parts, scale, weight, bias, cot, act, send):
    total = parts[0].astype(F32)
    for j in range(1, ROWS):
        total += parts[j].astype(F32)
    agg = (scale[...] * total).astype(BF16)
    pre = jnp.dot(agg, weight[...], preferred_element_type=F32) + bias[...]
    sigma = jax.nn.sigmoid(pre)
    act[...] = (pre * sigma).astype(BF16)
    grad_pre = cot[...].astype(F32) * sigma * (1.0 + pre * (1.0 - sigma))
    half = grad_pre.astype(BF16)
    grad_w = lax.dot_general(agg, half, (((0,), (0,)), ((), ())), preferred_element_type=F32)
    grad_b = jnp.sum(grad_pre, axis=0, keepdims=True)
    grad_b = jnp.concatenate([grad_b[:, :T], grad_b[:, T:]], axis=0)
    back = lax.dot_general(
        half, weight[...], (((1,), (1,)), ((), ())), preferred_element_type=F32
    )
    back = (scale[...] * back).astype(BF16)
    rows_b = bias_rows(grad_b)
    grad_w = grad_w.astype(BF16)
    for j in range(ROWS):
        send[j, 0:T] = back
        send[j, T : T + 16] = grad_w[16 * j : 16 * j + 16, :T]
        send[j, T + 16 : T + 32] = grad_w[16 * j : 16 * j + 16, T:]
        send[j, T + 32 : T + 48] = rows_b


def column_sums(meta, held, got, s, sums):
    sums[...] = jnp.zeros_like(sums)
    for i in range(ROWS):
        back = got[i, 0:T].T
        right = jnp.concatenate([held[i, s, c] for c in range(SLOTS)], axis=1)
        prod = jnp.dot(back, right, preferred_element_type=F32)
        for c in range(SLOTS):
            part = prod[:, c * T : (c + 1) * T]
            sums[tile_id(meta, i, s, c)] += part


def near_sums_kernel(meta, held, got, near, last, sums):
    total = got[0, T:].astype(F32)
    for j in range(1, ROWS):
        total += got[j, T:].astype(F32)
    total = jnp.concatenate(
        [total[0:32], total[32:34] + total[34:36], jnp.zeros((14, T), F32)], axis=0
    )
    high = total.astype(BF16)
    last[NODES : NODES + GRAD] = high
    last[NODES + GRAD :] = (total - high.astype(F32)).astype(BF16)
    column_sums(meta, held, got, 1 + 2 * meta[7, 0, 0], sums)
    last[0:NODES] = sums[0:ROWS].astype(BF16).reshape(NODES, T)
    column_sums(meta, held, got, 3 - 2 * meta[7, 0, 0], sums)
    near[...] = sums[0:ROWS].astype(BF16)


def far_sums_kernel(meta, held, got, far, sums):
    column_sums(meta, held, got, 2, sums)
    far[...] = sums[0:ROWS].astype(BF16)


def own_sums_kernel(meta, held, got, out, sums):
    column_sums(meta, held, got, 0, sums)
    out[...] = sums[0:ROWS]


def grads_of(rows):
    return rows[NODES : NODES + GRAD].astype(F32) + rows[NODES + GRAD :].astype(F32)


def near_kernel(far, other, out):
    for j in range(ROWS):
        rows = other[j * T : (j + 1) * T].astype(F32)
        out[j] = (far[j].astype(F32) + rows).astype(BF16)


def pair_kernel(mine, other, grads):
    grads[...] = grads_of(mine) + grads_of(other)


def group_kernel(grads, one, two, three, low, high, out):
    out[...] = (grads[...] + one[...]) + (two[...] + three[...])


def total_kernel(own, near, far, low, high):
    for half, first in ((low, 0), (high, HALF)):
        rows = pl.ds(first, HALF)
        total = own[rows] + near[rows].astype(F32) + far[rows].astype(F32)
        half[...] = total.astype(BF16)


def gather_kernel(low, high, grads, out):
    mine = grads[0:32].astype(BF16)
    for j in range(ROWS):
        out[j, 0:T] = low[j] if j < HALF else high[j - HALF]
        out[j, T:] = mine


def last_kernel(got, scale, grads, grad_features, grad_weight, grad_bias):
    total = got[0, 0:T].astype(F32)
    for j in range(1, ROWS):
        total += got[j, 0:T].astype(F32)
    grad_features[...] = scale[...] * total.T
    for j in range(ROWS):
        rows = slice(16 * j, 16 * j + 16)
        grad_weight[rows, :T] = got[j, T : T + 16].astype(F32)
        grad_weight[rows, T:] = got[j, T + 16 :].astype(F32)
    grad_bias[...] = jnp.concatenate([grads[32:33], grads[33:34]], axis=1)


def call(kernel, out, in_specs, scratch=(), flops=0, moved=1 << 20):
    return pl.pallas_call(
        kernel,
        out_shape=[jax.ShapeDtypeStruct(*o) for o in out],
        in_specs=in_specs,
        out_specs=[VMEM] * len(out),
        scratch_shapes=list(scratch),
        cost_estimate=pl.CostEstimate(flops=flops, bytes_accessed=moved, transcendentals=0),
        compiler_params=PARAMS,
    )


def pinned(value):
    return pltpu.with_memory_space_constraint(value, pltpu.HBM)


def exchange(value, axes):
    return lax.all_to_all(value, axes, 0, 0, tiled=True)


def move(value, to):
    blk, rep = Z * YL * CORE, X * YH
    pairs = []
    for b in range(blk):
        for r in range(rep):
            to_b, to_r = to(b, r)
            pairs.append((b * rep + r, to_b % blk * rep + to_r % rep))
    return lax.ppermute(value, BLK + REP, pairs)


def column(r):
    return r ^ (6 if r % 2 else 4)


def far_out(b, r):
    return (b + 2, r) if b % 4 < 2 else (b - 2, r - 1)


def far_back(b, r):
    return (b - 2, r) if b % 4 >= 2 else (b + 2, r + 1)


def swap(value, bit):
    return move(value, lambda b, r: (b ^ bit, r))


def on_device(features, degrees, cols, counts, edges, weight, bias, cot):
    z, yl, core = (lax.axis_index(a) for a in BLK)
    rep = lax.axis_index(REP)
    place = lax.broadcasted_iota(jnp.int32, (1, STEPS, ROWS), 2)
    place = jnp.where(place == 0, core, 0)
    meta = jnp.concatenate([cols.transpose(2, 1, 0), counts.T[None], place], axis=0)

    tiles, half = (ROWS, T, T), (HALF, T, T)
    low, high, scale = call(
        prologue_kernel,
        [(half, BF16), (half, BF16), ((T, T), F32)],
        [SMEM, VMEM, VMEM],
    )(rep.astype(jnp.int32)[None], pinned(features), pinned(degrees.reshape(ROWS, T)))

    low = move(low, lambda b, r: (b + 4 * r, r))
    high = move(high, lambda b, r: (b + 4 * column(r), column(r)))
    (held,) = call(
        load_kernel, [(edges.shape, BF16)], [HBM], [pltpu.SemaphoreType.DMA], 0, 12 << 20
    )(pinned(edges))
    low, held, meta = lax.optimization_barrier((low, held, meta))
    far_low, far_high = (move(v, far_out) for v in (low, high))
    near_low = move(low, lambda b, r: (b + 1 + 2 * (b % 2), r))

    work = 2 * ROWS * SLOTS * T * T * T
    block = pltpu.VMEM((ROWS + 1, T, T), BF16)
    (total,) = call(first_kernel, [(tiles, F32)], [SMEM] + [VMEM] * 3, [block], work, 3 << 20)(
        meta, held, low, high
    )
    high, total = lax.optimization_barrier((high, total))
    near_high = move(high, lambda b, r: (b + 1 + 2 * (b % 2), r))
    last_low, last_high = swap(far_low, 1), swap(far_high, 1)
    (total,) = call(second_kernel, [(tiles, F32)], [SMEM] + [VMEM] * 4, [block], work, 3 << 20)(
        meta, held, far_low, far_high, total
    )
    (parts,) = call(third_kernel, [(tiles, BF16)], [SMEM] + [VMEM] * 6, [block] * 2, 2 * work, 6 << 20)(
        meta, held, near_low, near_high, last_low, last_high, total
    )
    parts = exchange(parts, REP)

    act, send = call(
        dense_kernel,
        [(cot.shape, BF16), ((ROWS, T + GRAD, T), BF16)],
        [VMEM] * 5,
    )(parts, scale, weight, bias[None], cot)
    got = exchange(send, REP)

    sums = [pltpu.VMEM((ROWS + 1, T, T), F32)]
    near, mine = call(
        near_sums_kernel,
        [(tiles, BF16), ((NODES + 2 * GRAD, T), BF16)],
        [SMEM, VMEM, VMEM],
        sums,
        2 * work,
        6 << 20,
    )(meta, held, got)
    other = swap(mine, 1)
    near = move(near, lambda b, r: (b - 3 + 2 * (b % 2), r))
    (far,) = call(far_sums_kernel, [(tiles, BF16)], [SMEM, VMEM, VMEM], sums, work, 3 << 20)(
        meta, held, got
    )
    (far,) = call(near_kernel, [(tiles, BF16)], [VMEM] * 2)(far, other)
    far, got, other = lax.optimization_barrier((far, got, other))
    far = move(far, far_back)
    (own,) = call(own_sums_kernel, [(tiles, F32)], [SMEM] + [VMEM] * 2, sums, work, 3 << 20)(
        meta, held, got
    )
    (grads,) = call(pair_kernel, [((GRAD, T), F32)], [VMEM] * 2, (), PAIR_FLOPS)(mine, other)
    groups = [swap(grads, bits) for bits in (4, 8, 12)]
    low, high = call(total_kernel, [(half, BF16), (half, BF16)], [VMEM] * 3)(own, near, far)
    sent_low, sent_high = low, high
    low = move(low, lambda b, r: (b - 4 * r, r))
    high = move(high, lambda b, r: (b - 4 * r, r ^ 2))
    anywhere = pl.BlockSpec(memory_space=pl.ANY)
    (grads,) = call(
        group_kernel, [((GRAD, T), F32)], [VMEM] * 4 + [anywhere] * 2, (), GROUP_FLOPS
    )(grads, *groups, sent_low, sent_high)
    for bit in (2, 16):
        grads = grads + swap(grads, bit)
    (send,) = call(gather_kernel, [((ROWS, T + 32, T), BF16)], [VMEM] * 3)(low, high, grads)
    got = exchange(send, REP)
    grad_features, grad_weight, grad_bias = call(
        last_kernel,
        [((T, T), F32), ((T, 2 * T), F32), ((1, 2 * T), F32)],
        [VMEM] * 3,
    )(got, scale, grads)
    return act, grad_weight, grad_bias[0], grad_features


def solution(mesh):
    fine = Mesh(mesh.devices.reshape(Z, YL, CORE, X, YH), BLK + REP)
    return jax.shard_map(
        on_device,
        mesh=fine,
        in_specs=(
            P(BLK, None),
            P(BLK),
            P(BLK, REP, None),
            P(BLK, REP),
            P(BLK, REP, None, None, None),
            P(),
            P(),
            P(BLK + REP, None),
        ),
        out_specs=(P(BLK + REP, None), P(), P(), P(BLK + REP, None)),
        check_vma=False,
    )
```
